32 devices in a mesh: parts: 1, rows: 8 (over z, y), branch: 2 (over core), head: 2 (over x).
Axes of the slice: x: 2, y: 2, z: 4, core: 2. Of those that a mesh axis runs over, the one named last changes fastest.
Arguments:
- lineup_state: bfloat16 [32, 128, 256], P(('parts', 'rows', 'branch')), may hold values from -12 to 12
- pairwise: bfloat16 [128, 128, 128], P(('parts', 'rows', 'branch')), may hold values from -12 to 12
- aligned_residue_bounds: int32 [32, 2], P('parts'), may hold values from 0 to 128, as said below
- residue_valid_mask: int32 [128], P('parts'), may hold values from 0 to 1, as said below
- coupling_offset_weight_map: bfloat16 [128, 8], P(None, 'head'), may hold values from -0.5 to 0.5
- triangle_bias_matrix: bfloat16 [128, 4], P(None, 'head'), may hold values from -0.5 to 0.5
- alignment_projection_matrix: bfloat16 [4, 256, 256], P(None, None, 'head'), may hold values from -1 to 1
- lineup_readout_weight: bfloat16 [256, 256], replicated, may hold values from -4 to 4
- feedfwd_entry_weight: bfloat16 [256, 1024], P(None, 'head'), may hold values from -0.375 to 0.375
- feedfwd_exit_weight: bfloat16 [1024, 256], P('head'), may hold values from -0.1875 to 0.1875
- pair_projection_matrix: bfloat16 [4, 128, 128], P(None, None, 'head'), may hold values from -2 to 2
- pair_output_matrix: bfloat16 [128, 128], P(None, 'head'), may hold values from -6 to 6
- left_right_maps: bfloat16 [2, 256, 32], replicated, may hold values from -0.375 to 0.375
- outer_product_output_matrix: bfloat16 [1024, 128], P(None, 'head'), may hold values from -1.5 to 1.5
Outputs:
- refreshed_lineup_state: bfloat16 [32, 128, 256], P(('parts', 'rows', 'branch'), None, 'head')
- pairwise_out: bfloat16 [128, 128, 128], P(('parts', 'rows', 'branch'), None, 'head')
The draws below stay inside these ranges and needn't reach their ends.
Inputs may be any that keep to these rules, and one draw needn't show every extreme that they name: `aligned_residue_bounds`: each row holds a start below its end; row 0 covers all 128 residues; every span covers a quarter of the 128 residues or more and starts in the first half. `residue_valid_mask`: 1 on a prefix that holds at least half of the 128 residues, 0 after it; the last residue is always 0.
All inputs are finite; a program needn't handle non-finite values.
Results may differ from the reference program's by a relative error of at most 0.011.
Values may be sent and summed in bfloat16 or wider, within the bound.
A program may use at most 64 MiB of HBM per device.

```python
import math
import jax
import jax.numpy as jnp
from jax import lax

LINEUP_DEPTH = 256
COUPLING_DEPTH = 128
LINEUP_FOCI = 8
HZ = 4
PER_FOCUS_DIM = 32
OPM_DEPTH = 32
FEEDFWD_UNITS = 1024
LINEUP_STRANDS = 32
CHAIN_SPAN = 128


def raised_strands(key, lead, width):
    noise = jax.random.truncated_normal(jax.random.fold_in(key, 31), -6.0, 6.0, (lead, CHAIN_SPAN, width), jnp.float32)
    return noise


def raised_coefficient(key, width, features):
    base = jax.random.truncated_normal(jax.random.fold_in(key, 41), -4.0, 4.0, (4, width, features), jnp.float32) * width ** (-0.5)
    return base


def draw_lineup_state(key, part):
    return raised_strands(jax.random.fold_in(key, 5), LINEUP_STRANDS, LINEUP_DEPTH).astype(jnp.bfloat16)


def draw_pairwise(key, part):
    return raised_strands(jax.random.fold_in(key, 7), CHAIN_SPAN, COUPLING_DEPTH).astype(jnp.bfloat16)


def draw_alignment_projection_matrix(key, part):
    return raised_coefficient(jax.random.fold_in(key, 13), LINEUP_DEPTH, LINEUP_FOCI * PER_FOCUS_DIM).astype(jnp.bfloat16)


def draw_pair_projection_matrix(key, part):
    return raised_coefficient(jax.random.fold_in(key, 17), COUPLING_DEPTH, HZ * PER_FOCUS_DIM).astype(jnp.bfloat16)


def draw_aligned_residue_bounds(key, part):
    opening_draw_seed, closing_draw_seed = jax.random.split(jax.random.fold_in(key, 11))
    stretch_begin = jax.random.randint(opening_draw_seed, (LINEUP_STRANDS,), 0, CHAIN_SPAN // 2)
    stretch_extent = jax.random.randint(closing_draw_seed, (LINEUP_STRANDS,), CHAIN_SPAN // 4, CHAIN_SPAN + 1)
    span_end = jnp.minimum(stretch_begin + stretch_extent, CHAIN_SPAN)
    stretch_begin = stretch_begin.at[0].set(0)
    span_end = span_end.at[0].set(CHAIN_SPAN)
    return jnp.stack([stretch_begin, span_end], axis=1).astype(jnp.int32)


def draw_residue_valid_mask(key, part):
    valid_count = jax.random.randint(jax.random.fold_in(key, 23), (), CHAIN_SPAN // 2, CHAIN_SPAN)
    return (jnp.arange(CHAIN_SPAN, dtype=jnp.int32) < valid_count).astype(jnp.int32)


def level_of(own_key, shape, pieces, smallest, high):
    def one(axis_at, blocks):
        draws = jax.random.uniform(jax.random.fold_in(jax.random.fold_in(own_key, 6), axis_at), (blocks,), jnp.float32, smallest / len(pieces), high / len(pieces))
        return jnp.repeat(jnp.exp(draws), shape[axis_at] // blocks).reshape((-1,) + (1,) * (len(shape) - axis_at - 1))

    gain = one(*pieces[0])
    for cut in pieces[1:]:
        gain = gain * one(*cut)
    return gain


def bell_draw(own_key, dims, scale, reach, cuts=(), held_as=jnp.bfloat16):
    drawn = scale * jax.random.normal(own_key, dims, jnp.float32)
    if cuts:
        drawn = drawn * level_of(own_key, dims, cuts, -0.22, 0.18)
    return jnp.clip(drawn, -reach, reach).astype(held_as)


def setup_inputs(seed: int = 0, part: int = 0) -> dict:
    streams_of = jax.random.split(jax.random.key(seed), 15)
    part_keys = jax.random.split(jax.random.fold_in(streams_of[14], part), 15)
    return {
        "lineup_state": draw_lineup_state(jax.random.fold_in(jax.random.fold_in(streams_of[14], part), 71), part),
        "pairwise": draw_pairwise(jax.random.fold_in(jax.random.fold_in(streams_of[14], part), 71), part),
        "aligned_residue_bounds": draw_aligned_residue_bounds(jax.random.fold_in(jax.random.fold_in(streams_of[14], part), 71), part),
        "residue_valid_mask": draw_residue_valid_mask(jax.random.fold_in(jax.random.fold_in(streams_of[14], part), 71), part),
        "coupling_offset_weight_map": bell_draw(streams_of[4], (COUPLING_DEPTH, LINEUP_FOCI), COUPLING_DEPTH ** -0.5, 0.5, ((1, 2),)),
        "triangle_bias_matrix": bell_draw(streams_of[5], (COUPLING_DEPTH, HZ), COUPLING_DEPTH ** -0.5, 0.5, ((1, 2),)),
        "alignment_projection_matrix": draw_alignment_projection_matrix(jax.random.fold_in(streams_of[14], 71), part),
        "lineup_readout_weight": bell_draw(streams_of[7], (LINEUP_FOCI * PER_FOCUS_DIM, LINEUP_DEPTH), (max(1, LINEUP_FOCI * PER_FOCUS_DIM // 128)) ** -0.5, 4.0),
        "feedfwd_entry_weight": bell_draw(streams_of[8], (LINEUP_DEPTH, FEEDFWD_UNITS), LINEUP_DEPTH ** -0.5, 0.375, ((1, 2),)),
        "feedfwd_exit_weight": bell_draw(streams_of[9], (FEEDFWD_UNITS, LINEUP_DEPTH), FEEDFWD_UNITS ** -0.5, 0.1875, ((0, 2),)),
        "pair_projection_matrix": draw_pair_projection_matrix(jax.random.fold_in(streams_of[14], 71), part),
        "pair_output_matrix": bell_draw(streams_of[11], (HZ * PER_FOCUS_DIM, COUPLING_DEPTH), (max(1, HZ * PER_FOCUS_DIM // 128)) ** -0.5, 6.0, ((1, 2),)),
        "left_right_maps": bell_draw(streams_of[12], (2, LINEUP_DEPTH, OPM_DEPTH), LINEUP_DEPTH ** -0.5, 0.375),
        "outer_product_output_matrix": bell_draw(streams_of[13], (OPM_DEPTH * OPM_DEPTH, COUPLING_DEPTH), (OPM_DEPTH * OPM_DEPTH // 64) ** -0.5, 1.5, ((1, 2),)),
    }


def layer_normalize(values):
    values = values.astype(jnp.float32)
    center = values - lax.optimization_barrier(jnp.mean(values, -1, keepdims=True))
    spread = lax.optimization_barrier(jnp.mean(center * center, -1, keepdims=True))
    return center * lax.rsqrt(spread + 1e-05)

def soft_weights(attention_scores):
    row_max = lax.optimization_barrier(jnp.max(attention_scores, -1, keepdims=True))
    shifted = jnp.exp(attention_scores - row_max)
    return shifted / lax.optimization_barrier(jnp.sum(shifted, -1, keepdims=True))

def reference(lineup_state, pairwise, aligned_residue_bounds, residue_valid_mask, coupling_offset_weight_map, triangle_bias_matrix, alignment_projection_matrix, lineup_readout_weight, feedfwd_entry_weight, feedfwd_exit_weight, pair_projection_matrix, pair_output_matrix, left_right_maps, outer_product_output_matrix):
    places = jnp.arange(CHAIN_SPAN, dtype=jnp.int32)
    inside = (places[None, :] >= aligned_residue_bounds[:, 0:1]) & (places[None, :] < aligned_residue_bounds[:, 1:2])
    sequence_mask = inside.astype(jnp.float32)
    key_valid = residue_valid_mask > 0
    inv_scale = 1.0 / math.sqrt(PER_FOCUS_DIM)
    alignment_normed = layer_normalize(lineup_state).astype(jnp.bfloat16)
    pair_normed = layer_normalize(pairwise).astype(jnp.bfloat16)
    alignment_bias = jnp.einsum('tue,el->ltu', pair_normed.astype(jnp.float32), coupling_offset_weight_map.astype(jnp.float32)).astype(jnp.bfloat16)
    tri_bias = jnp.einsum('tue,el->ltu', pair_normed.astype(jnp.float32), triangle_bias_matrix.astype(jnp.float32)).astype(jnp.bfloat16)
    lineup_mapped = jnp.einsum('tvf,xfp->xtvp', alignment_normed.astype(jnp.float32), alignment_projection_matrix.astype(jnp.float32))
    lineup_probe_lookup_content = lineup_mapped[:3].astype(jnp.bfloat16).reshape(3, LINEUP_STRANDS, CHAIN_SPAN, LINEUP_FOCI, PER_FOCUS_DIM)
    alignment_gate = jax.nn.sigmoid(lineup_mapped[3])

    def alignment_row(row_elements):
        row_query, row_key, strand_content, gate_row, mask_row = row_elements
        attention_scores = jnp.einsum('ihd,jhd->hij', row_query.astype(jnp.float32), row_key.astype(jnp.float32)) * inv_scale
        attention_scores = attention_scores + alignment_bias.astype(jnp.float32)
        attention_scores = jnp.where(mask_row[None, None, :] > 0, attention_scores, -1000000000.0)
        softmax_shares = soft_weights(attention_scores).astype(jnp.bfloat16)
        mixed_strand = jnp.einsum('ftv,vfn->tfn', softmax_shares.astype(jnp.float32), strand_content.astype(jnp.float32)).reshape(CHAIN_SPAN, LINEUP_FOCI * PER_FOCUS_DIM)
        return (mixed_strand * gate_row).astype(jnp.bfloat16)
    lineup_focus_split = lax.map(alignment_row, (lineup_probe_lookup_content[0], lineup_probe_lookup_content[1], lineup_probe_lookup_content[2], alignment_gate, sequence_mask))
    lineup_blended = lineup_state.astype(jnp.float32) + jnp.dot(lineup_focus_split.reshape(LINEUP_STRANDS * CHAIN_SPAN, LINEUP_FOCI * PER_FOCUS_DIM), lineup_readout_weight, preferred_element_type=jnp.float32).reshape(LINEUP_STRANDS, CHAIN_SPAN, LINEUP_DEPTH)
    feedfwd_standardized = layer_normalize(lineup_blended).astype(jnp.bfloat16)
    feedfwd_inner = jax.nn.relu(jnp.dot(feedfwd_standardized.reshape(LINEUP_STRANDS * CHAIN_SPAN, LINEUP_DEPTH), feedfwd_entry_weight, preferred_element_type=jnp.float32)).astype(jnp.bfloat16)
    refreshed_lineup_state = (lineup_blended + jnp.dot(feedfwd_inner, feedfwd_exit_weight, preferred_element_type=jnp.float32).reshape(LINEUP_STRANDS, CHAIN_SPAN, LINEUP_DEPTH)).astype(jnp.bfloat16)

    def tri_row(z_row):
        row_proj = jnp.einsum('jc,gcd->gjd', z_row.astype(jnp.float32), pair_projection_matrix.astype(jnp.float32))
        row_qkv = row_proj[:3].astype(jnp.bfloat16).reshape(3, CHAIN_SPAN, HZ, PER_FOCUS_DIM)
        attention_scores = jnp.einsum('jhd,khd->hjk', row_qkv[0].astype(jnp.float32), row_qkv[1].astype(jnp.float32)) * inv_scale
        attention_scores = attention_scores + tri_bias.astype(jnp.float32)
        attention_scores = jnp.where(key_valid[None, None, :], attention_scores, -1000000000.0)
        softmax_shares = soft_weights(attention_scores).astype(jnp.bfloat16)
        mixed_strand = jnp.einsum('hjk,khd->jhd', softmax_shares.astype(jnp.float32), row_qkv[2].astype(jnp.float32)).reshape(CHAIN_SPAN, HZ * PER_FOCUS_DIM)
        return (mixed_strand * jax.nn.sigmoid(row_proj[3])).astype(jnp.bfloat16)
    pairwise_heads = lax.map(tri_row, pair_normed)
    tri_update = jnp.dot(pairwise_heads.reshape(CHAIN_SPAN * CHAIN_SPAN, HZ * PER_FOCUS_DIM), pair_output_matrix, preferred_element_type=jnp.float32).reshape(CHAIN_SPAN, CHAIN_SPAN, COUPLING_DEPTH)
    outer_factors = (jnp.einsum('juf,bfn->bjun', alignment_normed.astype(jnp.float32), left_right_maps.astype(jnp.float32)) * sequence_mask[None, :, :, None]).astype(jnp.bfloat16)
    pair_count = jnp.dot(sequence_mask.T, sequence_mask, precision=lax.Precision.HIGHEST)
    col_factors = outer_factors[1].astype(jnp.float32)

    def opm_row(row_elements):
        row_factor, counts = row_elements
        outer_sum = jnp.einsum('sp,sjq->jpq', row_factor.astype(jnp.float32), col_factors)
        outer_mean = (outer_sum / counts[:, None, None]).astype(jnp.bfloat16)
        return jnp.dot(outer_mean.reshape(CHAIN_SPAN, OPM_DEPTH * OPM_DEPTH), outer_product_output_matrix, preferred_element_type=jnp.float32)
    opm_update = lax.map(opm_row, (jnp.transpose(outer_factors[0], (1, 0, 2)), pair_count))
    pairwise_out = (pairwise.astype(jnp.float32) + tri_update + opm_update).astype(jnp.bfloat16)
    return (refreshed_lineup_state, pairwise_out)
```

```python
import functools
import math

import jax
import jax.numpy as jnp
from jax import lax
from jax.experimental import pallas as pl
from jax.experimental.pallas import tpu as pltpu
from jax.sharding import PartitionSpec as P

PER_FOCUS_DIM = 32


def layer_normalize(values):
    values = values.astype(jnp.float32)
    center = values - jnp.mean(values, -1, keepdims=True)
    spread = jnp.mean(center * center, -1, keepdims=True)
    return center * lax.rsqrt(spread + 1e-05)


def soft_weights(attention_scores):
    row_max = jnp.max(attention_scores, -1, keepdims=True)
    shifted = jnp.exp(attention_scores - row_max)
    return (shifted / jnp.sum(shifted, -1, keepdims=True)).astype(jnp.bfloat16)


def span_mask(aligned_residue_bounds, length_value):
    places = jnp.arange(length_value, dtype=jnp.int32)
    inside = (places[None, :] >= aligned_residue_bounds[:, 0:1]) & (
        places[None, :] < aligned_residue_bounds[:, 1:2]
    )
    return inside.astype(jnp.float32)


def local(
    lineup_state,
    pairwise,
    aligned_residue_bounds,
    residue_valid_mask,
    coupling_offset_weight_map,
    triangle_bias_matrix,
    alignment_projection_matrix,
    lineup_readout_weight,
    feedfwd_entry_weight,
    feedfwd_exit_weight,
    pair_projection_matrix,
    pair_output_matrix,
    left_right_maps,
    outer_product_output_matrix,
):
    sequence_shard_count = lineup_state.shape[0]
    length_value = lineup_state.shape[1]
    residue_shard_count = pairwise.shape[0]
    alignment_heads_sharded = coupling_offset_weight_map.shape[1]
    pairwise_heads_sharded = triangle_bias_matrix.shape[1]
    inv_scale = 1.0 / math.sqrt(PER_FOCUS_DIM)
    row_place = lax.axis_index(("rows", "branch"))
    head_location = lax.axis_index("head")
    seq_start = row_place * sequence_shard_count
    row_start = row_place * residue_shard_count
    mask_full = span_mask(aligned_residue_bounds, length_value)
    mask_own = lax.dynamic_slice_in_dim(mask_full, seq_start, sequence_shard_count, 0)
    key_valid = residue_valid_mask > 0
    alignment_normed = layer_normalize(lineup_state).astype(jnp.bfloat16)
    pair_normed = layer_normalize(pairwise).astype(jnp.bfloat16)
    bias_matrix = jnp.concatenate([coupling_offset_weight_map, triangle_bias_matrix], axis=1)
    bias_local = jnp.einsum(
        "tue,el->ltu", pair_normed, bias_matrix, preferred_element_type=jnp.float32
    ).astype(jnp.bfloat16)
    lineup_mapped = jnp.einsum(
        "tvf,xfp->xtvp",
        alignment_normed,
        alignment_projection_matrix,
        preferred_element_type=jnp.float32,
    )
    lineup_probe_lookup_content = (
        lineup_mapped[:3]
        .astype(jnp.bfloat16)
        .reshape(3, sequence_shard_count, length_value, alignment_heads_sharded, PER_FOCUS_DIM)
    )
    alignment_gate = jax.nn.sigmoid(lineup_mapped[3])
    pair_proj = jnp.einsum(
        "ijc,gcd->gijd", pair_normed, pair_projection_matrix, preferred_element_type=jnp.float32
    )
    pair_qkv = (
        pair_proj[:3]
        .astype(jnp.bfloat16)
        .reshape(3, residue_shard_count, length_value, pairwise_heads_sharded, PER_FOCUS_DIM)
    )
    pair_gate = jax.nn.sigmoid(pair_proj[3])
    bias_portion = lax.all_gather(bias_local, ("rows", "branch"), axis=1, tiled=True)
    row_total_count = bias_portion.shape[1]
    alignment_query = lineup_probe_lookup_content[0]
    attention_scores = (
        jnp.einsum(
            "xtza,xfza->xztf",
            alignment_query,
            lineup_probe_lookup_content[1],
            preferred_element_type=jnp.float32,
        )
        * inv_scale
    )
    attention_scores = (
        attention_scores + bias_portion[:alignment_heads_sharded].astype(jnp.float32)[None]
    )
    attention_scores = jnp.where(mask_own[:, None, None, :] > 0, attention_scores, -1000000000.0)
    softmax_shares = soft_weights(attention_scores)
    alignment_portion = jnp.einsum(
        "fxkc,fcxz->fkxz",
        softmax_shares,
        lineup_probe_lookup_content[2],
        preferred_element_type=jnp.float32,
    )
    alignment_portion = alignment_portion.reshape(
        sequence_shard_count, row_total_count, alignment_heads_sharded * PER_FOCUS_DIM
    )
    alignment_portion = (alignment_portion * alignment_gate).astype(jnp.bfloat16)
    pair_query = pair_qkv[0]
    triangle_scores = (
        jnp.einsum("ijhd,ikhd->ihjk", pair_query, pair_qkv[1], preferred_element_type=jnp.float32)
        * inv_scale
    )
    triangle_scores = (
        triangle_scores + bias_portion[alignment_heads_sharded:].astype(jnp.float32)[None]
    )
    triangle_scores = jnp.where(key_valid[None, None, None, :], triangle_scores, -1000000000.0)
    tri_weights = soft_weights(triangle_scores)
    pair_part = jnp.einsum(
        "ihjk,ikhd->ijhd", tri_weights, pair_qkv[2], preferred_element_type=jnp.float32
    )
    pair_part = pair_part.reshape(
        residue_shard_count, row_total_count, pairwise_heads_sharded * PER_FOCUS_DIM
    )
    pair_part = (pair_part * pair_gate).astype(jnp.bfloat16)
    alignment_flattened = jnp.transpose(alignment_portion, (1, 0, 2)).reshape(
        row_total_count, sequence_shard_count * alignment_heads_sharded * PER_FOCUS_DIM
    )
    pair_flattened = jnp.transpose(pair_part, (1, 0, 2)).reshape(
        row_total_count, residue_shard_count * pairwise_heads_sharded * PER_FOCUS_DIM
    )
    attention_result = jnp.concatenate([alignment_flattened, pair_flattened], axis=1)
    alignment_width = sequence_shard_count * alignment_heads_sharded * PER_FOCUS_DIM
    alignment_local = jnp.transpose(
        attention_result[:, :alignment_width].reshape(
            length_value, sequence_shard_count, alignment_heads_sharded * PER_FOCUS_DIM
        ),
        (1, 0, 2),
    )
    pair_local = jnp.transpose(
        attention_result[:, alignment_width:].reshape(
            length_value, residue_shard_count, pairwise_heads_sharded * PER_FOCUS_DIM
        ),
        (1, 0, 2),
    )
    lineup_focus_split, pairwise_heads = (
        lax.all_gather(alignment_local, "head", axis=2, tiled=True),
        lax.all_gather(pair_local, "head", axis=2, tiled=True),
    )
    outer_factors = jnp.einsum(
        "juf,bfn->bjun", alignment_normed, left_right_maps, preferred_element_type=jnp.float32
    )
    outer_factors = (outer_factors * mask_own[None, :, :, None]).astype(jnp.bfloat16)
    factor_rows = lax.all_to_all(
        outer_factors[0], ("rows", "branch"), split_axis=1, concat_axis=0, tiled=True
    )
    col_factors = lax.all_gather(outer_factors[1], ("rows", "branch"), axis=0, tiled=True)
    mask_rows = lax.dynamic_slice_in_dim(mask_full, row_start, residue_shard_count, 1)
    pair_count = jnp.dot(mask_rows.T, mask_full, precision=lax.Precision.HIGHEST)
    col_block = math.gcd(length_value, 128)

    def outer_block(col_start):
        block_cols = lax.dynamic_slice_in_dim(col_factors, col_start, col_block, 1)
        outer_sum = lax.dot_general(
            factor_rows, block_cols, (((0,), (0,)), ((), ())), preferred_element_type=jnp.float32
        )
        counts = lax.dynamic_slice_in_dim(pair_count, col_start, col_block, 1)
        outer_mean = (outer_sum / counts[:, None, :, None]).astype(jnp.bfloat16)
        outer_mean = jnp.transpose(outer_mean, (0, 2, 1, 3)).reshape(
            residue_shard_count * col_block, -1
        )
        return jnp.dot(
            outer_mean, outer_product_output_matrix, preferred_element_type=jnp.float32
        ).reshape(residue_shard_count, col_block, -1)

    starts = jnp.arange(length_value // col_block, dtype=jnp.int32) * col_block
    opm_blocks = lax.map(outer_block, starts)
    opm_update = jnp.transpose(opm_blocks, (1, 0, 2, 3)).reshape(
        residue_shard_count, length_value, -1
    )
    width_z = pair_output_matrix.shape[1]
    tri_update = jnp.dot(
        pairwise_heads.reshape(residue_shard_count * length_value, -1),
        pair_output_matrix,
        preferred_element_type=jnp.float32,
    ).reshape(residue_shard_count, length_value, width_z)
    pair_own = lax.dynamic_slice_in_dim(pairwise, head_location * width_z, width_z, 2).astype(
        jnp.float32
    )
    pairwise_out = (pair_own + tri_update + opm_update).astype(jnp.bfloat16)
    channels = lineup_state.shape[2]
    lineup_blended = lineup_state.astype(jnp.float32) + jnp.dot(
        lineup_focus_split.reshape(sequence_shard_count * length_value, -1),
        lineup_readout_weight,
        preferred_element_type=jnp.float32,
    ).reshape(sequence_shard_count, length_value, channels)
    feedfwd_standardized = layer_normalize(lineup_blended).astype(jnp.bfloat16)
    head_count = lax.axis_size("head")
    hidden = jax.nn.relu(
        jnp.einsum(
            "src,cf->srf",
            feedfwd_standardized,
            feedfwd_entry_weight,
            preferred_element_type=jnp.float32,
        )
    ).astype(jnp.bfloat16)
    partial_value = jnp.einsum(
        "srf,fc->src", hidden, feedfwd_exit_weight, preferred_element_type=jnp.float32
    )
    summed_result = lax.psum_scatter(
        partial_value.astype(jnp.bfloat16), "head", scatter_dimension=2, tiled=True
    ).astype(jnp.float32)
    alignment_channel_width = channels // head_count
    alignment_owned = lax.dynamic_slice_in_dim(
        lineup_blended, head_location * alignment_channel_width, alignment_channel_width, 2
    )
    refreshed_lineup_state = (alignment_owned + summed_result).astype(jnp.bfloat16)
    return (refreshed_lineup_state, pairwise_out)


F32 = jnp.float32
BF16 = jnp.bfloat16
NEG = -1000000000.0
HD = PER_FOCUS_DIM


def dot_nt(a, b):
    return lax.dot_general(a, b, (((1,), (1,)), ((), ())), preferred_element_type=F32)


def dot_nn(a, b):
    return jnp.dot(a, b, preferred_element_type=F32)


def head_mask(width, head):
    lanes = lax.broadcasted_iota(jnp.int32, (1, width), 1)
    return jnp.where((lanes >= head * HD) & (lanes < (head + 1) * HD), 1.0, 0.0)


def block_kernel(
    N,
    NB,
    S,
    R,
    L,
    x_ref,
    z_ref,
    bs_ref,
    bv_ref,
    val_ref,
    cw_ref,
    tw_ref,
    ap_ref,
    wr_ref,
    we_ref,
    wx_ref,
    pp_ref,
    po_ref,
    lr_ref,
    ow_ref,
    out_m,
    out_z,
    pn,
    xn,
    wscr,
    bscr,
    bias_all,
    b_all,
    a_send,
    a_all,
    bias_f,
    q_s,
    k_s,
    v_s,
    g_s,
    pq_s,
    pk_s,
    pv_s,
    pg_s,
    wf,
    wt,
    bf,
    bmat,
    af,
    at,
    omat,
    mh_own,
    mh_oth,
    ph_own,
    ph_oth,
    mid,
    ps_own,
    ps_send,
    ps_recv,
    bias_ss,
    bias_rs,
    b_ss,
    b_rs,
    a_ss,
    a_rs,
    m_ss,
    m_rs,
    p_ss,
    p_rs,
    f_ss,
    f_rs,
):
    part = lax.axis_index("parts")
    row = lax.axis_index("rows")
    core = lax.axis_index("branch")
    h = lax.axis_index("head")
    me = row * NB + core
    HM = cw_ref.shape[1]
    HZ = tw_ref.shape[1]
    H = HM + HZ
    Q = lr_ref.shape[2]
    C = po_ref.shape[1]
    DM = HM * HD
    DZ = HZ * HD
    inv = 1.0 / math.sqrt(HD)

    def peer(d):
        p = lax.rem(me + d, N)
        return p, (part, p // NB, lax.rem(p, NB), h)

    partner = (part, row, core, 1 - h)

    def remote(src, dst, ss, rs, dev):
        return pltpu.make_async_remote_copy(
            src_ref=src,
            dst_ref=dst,
            send_sem=ss,
            recv_sem=rs,
            device_id=dev,
            device_id_type=pl.DeviceIdType.MESH,
        )

    barrier = pltpu.get_barrier_semaphore()

    def greet(d, c):
        pl.semaphore_signal(
            barrier, inc=1, device_id=peer(d)[1], device_id_type=pl.DeviceIdType.MESH
        )
        return c

    lax.fori_loop(1, N, greet, 0)
    pl.semaphore_signal(barrier, inc=1, device_id=partner, device_id_type=pl.DeviceIdType.MESH)

    pn[...] = layer_normalize(z_ref[...]).astype(BF16)
    wscr[...] = jnp.zeros(wscr.shape, F32)
    wscr[0, :, 0:HM] = cw_ref[...].astype(F32)
    wscr[1, :, 0:HZ] = tw_ref[...].astype(F32)
    for t in range(2):
        w8 = wscr[t].T[0:8].astype(BF16)
        bt = dot_nt(w8, pn[...])
        for j in range(R):
            bscr[t, j * 8 : (j + 1) * 8, :] = bt[:, j * L : (j + 1) * L]
    pieces = [bscr[0, pl.ds(l, R, stride=8), :] for l in range(HM)]
    pieces += [bscr[1, pl.ds(l, R, stride=8), :] for l in range(HZ)]
    bias_all[me] = jnp.concatenate(pieces, 0).astype(BF16)

    pl.semaphore_wait(barrier, N)

    def send_bias(d, c):
        p, dev = peer(d)
        remote(bias_all.at[me], bias_all.at[me], bias_ss.at[p], bias_rs.at[me], dev).start()
        return c

    lax.fori_loop(1, N, send_bias, 0)

    xn[...] = layer_normalize(x_ref[...]).astype(BF16)
    lanes = lax.broadcasted_iota(jnp.int32, (1, L), 1)
    tall = lax.broadcasted_iota(jnp.int32, (L, 1), 0)
    ft = dot_nt(lr_ref[1].astype(F32).T.astype(BF16), xn[...])
    fa = dot_nn(xn[...], lr_ref[0])
    own_mask = []
    parts_a = []
    for s in range(S):
        lo = bs_ref[me * S + s, 0]
        hi = bs_ref[me * S + s, 1]
        inside = (lanes >= lo) & (lanes < hi)
        own_mask.append(inside)
        b_all[me, s * Q : (s + 1) * Q, :] = (
            ft[:, s * L : (s + 1) * L] * jnp.where(inside, 1.0, 0.0)
        ).astype(BF16)
        parts_a.append(
            fa[s * L : (s + 1) * L] * jnp.where((tall >= lo) & (tall < hi), 1.0, 0.0)
        )
    for p in range(N):
        a_send[p] = jnp.concatenate(
            [parts_a[s][p * R : (p + 1) * R] for s in range(S)], 0
        ).astype(BF16)
    a_all[me] = a_send[me]

    def send_factors(d, c):
        p, dev = peer(d)
        remote(b_all.at[me], b_all.at[me], b_ss.at[p], b_rs.at[me], dev).start()
        remote(a_send.at[p], a_all.at[me], a_ss.at[p], a_rs.at[me], dev).start()
        return c

    lax.fori_loop(1, N, send_factors, 0)

    for g, ref in ((0, q_s), (1, k_s), (2, v_s)):
        ref[...] = dot_nn(xn[...], ap_ref[g]).astype(BF16)
    g_s[...] = jax.nn.sigmoid(dot_nn(xn[...], ap_ref[3]))
    for g, ref in ((0, pq_s), (1, pk_s), (2, pv_s)):
        ref[...] = dot_nn(pn[...], pp_ref[g]).astype(BF16)
    pg_s[...] = jax.nn.sigmoid(dot_nn(pn[...], pp_ref[3]))

    wf[...] = ow_ref[...].astype(F32)
    for q in range(Q):
        wt[q * Q : (q + 1) * Q, :] = wf[pl.ds(q, Q, stride=Q), :].astype(BF16)

    alllanes = lax.broadcasted_iota(jnp.int32, (N * S, L), 1)
    lo_v = bv_ref[:, 0:1]
    hi_v = bv_ref[:, 1:2]
    m_all = jnp.where((alllanes >= lo_v) & (alllanes < hi_v), 1.0, 0.0)
    shifted = alllanes + me * R
    m_own = jnp.where((shifted >= lo_v) & (shifted < hi_v), 1.0, 0.0)
    counts = dot_nn(m_own.T[0:R].astype(BF16), m_all.astype(BF16))
    inv_counts = 1.0 / counts

    def wait_bias(d, c):
        p, dev = peer(d)
        remote(bias_all.at[p], bias_all.at[p], bias_ss.at[p], bias_rs.at[p], dev).wait_recv()
        return c

    lax.fori_loop(1, N, wait_bias, 0)
    valid = val_ref[...] > 0
    for p in range(N):
        piece = bias_all[p].astype(F32)
        for l in range(H):
            sub = piece[l * R : (l + 1) * R]
            if l >= HM:
                sub = jnp.where(valid, sub, NEG)
            bias_f[l * L + p * R : l * L + (p + 1) * R, :] = sub

    mm = [head_mask(DM, i).astype(BF16) for i in range(HM)]
    m_copies = []
    for s in range(S):
        sl = slice(s * L, (s + 1) * L)
        q = q_s[sl]
        v = v_s[sl]
        stack = jnp.concatenate([q * m for m in mm], 0)
        score = dot_nt(stack, k_s[sl]) * inv + bias_f[0 : HM * L, :]
        score = jnp.where(own_mask[s], score, NEG)
        w = jnp.exp(score - jnp.max(score, -1, keepdims=True)).astype(BF16)
        w = jnp.concatenate([w[i * L : (i + 1) * L] for i in range(HM)], 1)
        vv = jnp.concatenate(
            [jnp.concatenate([v * m, jnp.broadcast_to(m, v.shape)], 1) for m in mm], 0
        )
        o = dot_nn(w, vv)
        mh_own[sl] = (o[:, :DM] / o[:, DM:] * g_s[sl]).astype(BF16)
        copy = remote(mh_own.at[sl], mh_oth.at[sl], m_ss.at[s], m_rs.at[s], partner)
        copy.start()
        m_copies.append(copy)

    zm = [head_mask(DZ, i).astype(BF16) for i in range(HZ)]

    def tri(i):
        sl = slice(i * L, (i + 1) * L)
        q = pq_s[sl]
        v = pv_s[sl]
        stack = jnp.concatenate([q * m for m in zm], 0)
        score = dot_nt(stack, pk_s[sl]) * inv + bias_f[HM * L :, :]
        w = jnp.exp(score - jnp.max(score, -1, keepdims=True)).astype(BF16)
        w = jnp.concatenate([w[j * L : (j + 1) * L] for j in range(HZ)], 1)
        vv = jnp.concatenate(
            [jnp.concatenate([v * m, jnp.broadcast_to(m, v.shape)], 1) for m in zm], 0
        )
        o = dot_nn(w, vv)
        return o[:, :DZ] / o[:, DZ:] * pg_s[sl]

    half = R // 2
    p_copies = []
    for i in range(half):
        sl = slice(i * L, (i + 1) * L)
        ph_own[sl] = jnp.concatenate([tri(i), tri(i + half)], 1).astype(BF16)
        copy = remote(ph_own.at[sl], ph_oth.at[sl], p_ss.at[i], p_rs.at[i], partner)
        copy.start()
        p_copies.append(copy)

    for copy in m_copies:
        copy.wait_recv()
    w_own = wr_ref[pl.ds(pl.multiple_of(h * DM, DM), DM), :]
    w_oth = wr_ref[pl.ds(pl.multiple_of((1 - h) * DM, DM), DM), :]
    mid[...] = x_ref[...].astype(F32) + dot_nn(mh_own[...], w_own) + dot_nn(mh_oth[...], w_oth)
    tn = layer_normalize(mid[...]).astype(BF16)
    hidden = jnp.maximum(dot_nn(tn, we_ref[...]), 0.0).astype(BF16)
    W = out_m.shape[1]
    sums = dot_nn(hidden, wx_ref[...])
    first = h == 0
    ps_own[...] = jnp.where(first, sums[:, :W], sums[:, W:])
    ps_send[...] = jnp.where(first, sums[:, W:], sums[:, :W]).astype(BF16)
    f_copy = remote(ps_send, ps_recv, f_ss, f_rs, partner)
    f_copy.start()

    def wait_factors(d, c):
        p, dev = peer(d)
        remote(b_all.at[p], b_all.at[p], b_ss.at[p], b_rs.at[p], dev).wait_recv()
        remote(a_send.at[p], a_all.at[p], a_ss.at[p], a_rs.at[p], dev).wait_recv()
        return c

    lax.fori_loop(1, N, wait_factors, 0)
    SQ = S * Q
    SR = S * R
    for p in range(N):
        bf[p * SQ : (p + 1) * SQ, :] = b_all[p].astype(F32)
        af[p * SR : (p + 1) * SR, :] = a_all[p].astype(F32)
    for q in range(Q):
        bmat[:, q * L : (q + 1) * L] = bf[pl.ds(q, N * S, stride=Q), :].astype(BF16)
    for i in range(R):
        at[i * Q : (i + 1) * Q, :] = af[pl.ds(i, N * S, stride=R), :].T.astype(BF16)
    step = 8
    for q0 in range(0, Q, step):
        o = dot_nn(at[...], bmat[:, q0 * L : (q0 + step) * L]).astype(BF16)
        for q in range(step):
            for i in range(R):
                omat[(q0 + q) * Q : (q0 + q + 1) * Q, i * L : (i + 1) * L] = o[
                    i * Q : (i + 1) * Q, q * L : (q + 1) * L
                ]
    res = dot_nn(wt[...].astype(F32).T.astype(BF16), omat[...])

    zw = jnp.zeros((DZ, C), BF16)
    po = [po_ref[pl.ds(pl.multiple_of(t * DZ, DZ), DZ), :] for t in (h, 1 - h)]
    lowers = [jnp.concatenate([w, zw], 0) for w in po]
    uppers = [jnp.concatenate([zw, w], 0) for w in po]
    for copy in p_copies:
        copy.wait_recv()
    for i in range(R):
        k = i % half
        sl = slice(k * L, (k + 1) * L)
        ws = lowers if i < half else uppers
        tri_out = dot_nn(ph_own[sl], ws[0]) + dot_nn(ph_oth[sl], ws[1])
        opm = (res[:, i * L : (i + 1) * L] * inv_counts[i : i + 1, :]).T
        zi = z_ref[i * L : (i + 1) * L, :].astype(F32)
        base = jnp.where(first, zi[:, :C], zi[:, C:])
        out_z[i] = (base + tri_out + opm).astype(BF16)

    f_copy.wait_recv()
    out_m[...] = (
        mid[:, pl.ds(pl.multiple_of(h * W, W), W)] + ps_own[...] + ps_recv[...].astype(F32)
    ).astype(BF16)

    def drain(d, c):
        p, dev = peer(d)
        remote(bias_all.at[me], bias_all.at[me], bias_ss.at[p], bias_rs.at[me], dev).wait_send()
        remote(b_all.at[me], b_all.at[me], b_ss.at[p], b_rs.at[me], dev).wait_send()
        remote(a_send.at[p], a_all.at[me], a_ss.at[p], a_rs.at[me], dev).wait_send()
        return c

    lax.fori_loop(1, N, drain, 0)
    for copy in m_copies + p_copies + [f_copy]:
        copy.wait_send()


def fused(N, NB, *args):
    x, z, bounds, valid, cw, tw, ap, wr, we, wx, pp, po, lr, ow = args
    S, L, D = x.shape
    R, _, CZ = z.shape
    HM, HZ = cw.shape[1], tw.shape[1]
    H = HM + HZ
    Q = lr.shape[2]
    C = po.shape[1]
    DM, DZ = HM * HD, HZ * HD
    W = D // 2
    vmem = pl.BlockSpec(memory_space=pltpu.VMEM)
    smem = pl.BlockSpec(memory_space=pltpu.SMEM)
    dma = pltpu.SemaphoreType.DMA
    scratch = [
        pltpu.VMEM((R * L, CZ), BF16),
        pltpu.VMEM((S * L, D), BF16),
        pltpu.VMEM((2, CZ, 128), F32),
        pltpu.VMEM((2, R * 8, L), F32),
        pltpu.VMEM((N, H * R, L), BF16),
        pltpu.VMEM((N, S * Q, L), BF16),
        pltpu.VMEM((N, S * R, Q), BF16),
        pltpu.VMEM((N, S * R, Q), BF16),
        pltpu.VMEM((H * L, L), F32),
        pltpu.VMEM((S * L, DM), BF16),
        pltpu.VMEM((S * L, DM), BF16),
        pltpu.VMEM((S * L, DM), BF16),
        pltpu.VMEM((S * L, DM), F32),
        pltpu.VMEM((R * L, DZ), BF16),
        pltpu.VMEM((R * L, DZ), BF16),
        pltpu.VMEM((R * L, DZ), BF16),
        pltpu.VMEM((R * L, DZ), F32),
        pltpu.VMEM((Q * Q, C), F32),
        pltpu.VMEM((Q * Q, C), BF16),
        pltpu.VMEM((N * S * Q, L), F32),
        pltpu.VMEM((N * S, Q * L), BF16),
        pltpu.VMEM((N * S * R, Q), F32),
        pltpu.VMEM((R * Q, N * S), BF16),
        pltpu.VMEM((Q * Q, R * L), BF16),
        pltpu.VMEM((S * L, DM), BF16),
        pltpu.VMEM((S * L, DM), BF16),
        pltpu.VMEM((R // 2 * L, 2 * DZ), BF16),
        pltpu.VMEM((R // 2 * L, 2 * DZ), BF16),
        pltpu.VMEM((S * L, D), F32),
        pltpu.VMEM((S * L, W), F32),
        pltpu.VMEM((S * L, W), BF16),
        pltpu.VMEM((S * L, W), BF16),
        dma((N,)),
        dma((N,)),
        dma((N,)),
        dma((N,)),
        dma((N,)),
        dma((N,)),
        dma((S,)),
        dma((S,)),
        dma((R // 2,)),
        dma((R // 2,)),
        dma,
        dma,
    ]
    out_m, out_z = pl.pallas_call(
        functools.partial(block_kernel, N, NB, S, R, L),
        out_shape=(
            jax.ShapeDtypeStruct((S * L, W), BF16),
            jax.ShapeDtypeStruct((R, L, C), BF16),
        ),
        in_specs=[vmem, vmem, smem] + [vmem] * 12,
        out_specs=(vmem, vmem),
        scratch_shapes=scratch,
        compiler_params=pltpu.CompilerParams(
            collective_id=0, has_side_effects=True, vmem_limit_bytes=48 * 1024 * 1024
        ),
    )(
        x.reshape(S * L, D),
        z.reshape(R * L, CZ),
        bounds,
        bounds,
        valid.reshape(1, L),
        cw,
        tw,
        ap,
        wr,
        we,
        wx,
        pp,
        po,
        lr,
        ow,
    )
    return out_m.reshape(S, L, W), out_z


def block(N, NB, NH, *args):
    x, z = args[0], args[1]
    S, L, D = x.shape
    if NH == 2 and L == 128 and z.shape[0] == 8 and S == 2 and D == 256:
        return fused(N, NB, *args)
    return local(*args)


def solution(mesh):
    NB = mesh.shape["branch"]
    N = mesh.shape["rows"] * NB
    in_specs = (
        P(("parts", "rows", "branch"), None, None),
        P(("parts", "rows", "branch"), None, None),
        P("parts", None),
        P("parts"),
        P(None, "head"),
        P(None, "head"),
        P(None, None, "head"),
        P(),
        P(None, "head"),
        P("head", None),
        P(None, None, "head"),
        P(None, "head"),
        P(),
        P(None, "head"),
    )
    out_specs = (
        P(("parts", "rows", "branch"), None, "head"),
        P(("parts", "rows", "branch"), None, "head"),
    )
    return jax.shard_map(
        functools.partial(block, N, NB, mesh.shape["head"]), mesh=mesh, in_specs=in_specs, out_specs=out_specs, check_vma=False)
```

```python
import functools
import math

import jax
import jax.numpy as jnp
from jax import lax
from jax.experimental import pallas as pl
from jax.experimental.pallas import tpu as pltpu
from jax.sharding import PartitionSpec as P

PER_FOCUS_DIM = 32


def layer_normalize(values):
    values = values.astype(jnp.float32)
    center = values - jnp.mean(values, -1, keepdims=True)
    spread = jnp.mean(center * center, -1, keepdims=True)
    return center * lax.rsqrt(spread + 1e-05)


def soft_weights(attention_scores):
    row_max = jnp.max(attention_scores, -1, keepdims=True)
    shifted = jnp.exp(attention_scores - row_max)
    return (shifted / jnp.sum(shifted, -1, keepdims=True)).astype(jnp.bfloat16)


def span_mask(aligned_residue_bounds, length_value):
    places = jnp.arange(length_value, dtype=jnp.int32)
    inside = (places[None, :] >= aligned_residue_bounds[:, 0:1]) & (
        places[None, :] < aligned_residue_bounds[:, 1:2]
    )
    return inside.astype(jnp.float32)


def local(
    lineup_state,
    pairwise,
    aligned_residue_bounds,
    residue_valid_mask,
    coupling_offset_weight_map,
    triangle_bias_matrix,
    alignment_projection_matrix,
    lineup_readout_weight,
    feedfwd_entry_weight,
    feedfwd_exit_weight,
    pair_projection_matrix,
    pair_output_matrix,
    left_right_maps,
    outer_product_output_matrix,
):
    sequence_shard_count = lineup_state.shape[0]
    length_value = lineup_state.shape[1]
    residue_shard_count = pairwise.shape[0]
    alignment_heads_sharded = coupling_offset_weight_map.shape[1]
    pairwise_heads_sharded = triangle_bias_matrix.shape[1]
    inv_scale = 1.0 / math.sqrt(PER_FOCUS_DIM)
    row_place = lax.axis_index(("rows", "branch"))
    head_location = lax.axis_index("head")
    seq_start = row_place * sequence_shard_count
    row_start = row_place * residue_shard_count
    mask_full = span_mask(aligned_residue_bounds, length_value)
    mask_own = lax.dynamic_slice_in_dim(mask_full, seq_start, sequence_shard_count, 0)
    key_valid = residue_valid_mask > 0
    alignment_normed = layer_normalize(lineup_state).astype(jnp.bfloat16)
    pair_normed = layer_normalize(pairwise).astype(jnp.bfloat16)
    bias_matrix = jnp.concatenate([coupling_offset_weight_map, triangle_bias_matrix], axis=1)
    bias_local = jnp.einsum(
        "tue,el->ltu", pair_normed, bias_matrix, preferred_element_type=jnp.float32
    ).astype(jnp.bfloat16)
    lineup_mapped = jnp.einsum(
        "tvf,xfp->xtvp",
        alignment_normed,
        alignment_projection_matrix,
        preferred_element_type=jnp.float32,
    )
    lineup_probe_lookup_content = (
        lineup_mapped[:3]
        .astype(jnp.bfloat16)
        .reshape(3, sequence_shard_count, length_value, alignment_heads_sharded, PER_FOCUS_DIM)
    )
    alignment_gate = jax.nn.sigmoid(lineup_mapped[3])
    pair_proj = jnp.einsum(
        "ijc,gcd->gijd", pair_normed, pair_projection_matrix, preferred_element_type=jnp.float32
    )
    pair_qkv = (
        pair_proj[:3]
        .astype(jnp.bfloat16)
        .reshape(3, residue_shard_count, length_value, pairwise_heads_sharded, PER_FOCUS_DIM)
    )
    pair_gate = jax.nn.sigmoid(pair_proj[3])
    bias_portion = lax.all_gather(bias_local, ("rows", "branch"), axis=1, tiled=True)
    row_total_count = bias_portion.shape[1]
    alignment_query = lineup_probe_lookup_content[0]
    attention_scores = (
        jnp.einsum(
            "xtza,xfza->xztf",
            alignment_query,
            lineup_probe_lookup_content[1],
            preferred_element_type=jnp.float32,
        )
        * inv_scale
    )
    attention_scores = (
        attention_scores + bias_portion[:alignment_heads_sharded].astype(jnp.float32)[None]
    )
    attention_scores = jnp.where(mask_own[:, None, None, :] > 0, attention_scores, -1000000000.0)
    softmax_shares = soft_weights(attention_scores)
    alignment_portion = jnp.einsum(
        "fxkc,fcxz->fkxz",
        softmax_shares,
        lineup_probe_lookup_content[2],
        preferred_element_type=jnp.float32,
    )
    alignment_portion = alignment_portion.reshape(
        sequence_shard_count, row_total_count, alignment_heads_sharded * PER_FOCUS_DIM
    )
    alignment_portion = (alignment_portion * alignment_gate).astype(jnp.bfloat16)
    pair_query = pair_qkv[0]
    triangle_scores = (
        jnp.einsum("ijhd,ikhd->ihjk", pair_query, pair_qkv[1], preferred_element_type=jnp.float32)
        * inv_scale
    )
    triangle_scores = (
        triangle_scores + bias_portion[alignment_heads_sharded:].astype(jnp.float32)[None]
    )
    triangle_scores = jnp.where(key_valid[None, None, None, :], triangle_scores, -1000000000.0)
    tri_weights = soft_weights(triangle_scores)
    pair_part = jnp.einsum(
        "ihjk,ikhd->ijhd", tri_weights, pair_qkv[2], preferred_element_type=jnp.float32
    )
    pair_part = pair_part.reshape(
        residue_shard_count, row_total_count, pairwise_heads_sharded * PER_FOCUS_DIM
    )
    pair_part = (pair_part * pair_gate).astype(jnp.bfloat16)
    alignment_flattened = jnp.transpose(alignment_portion, (1, 0, 2)).reshape(
        row_total_count, sequence_shard_count * alignment_heads_sharded * PER_FOCUS_DIM
    )
    pair_flattened = jnp.transpose(pair_part, (1, 0, 2)).reshape(
        row_total_count, residue_shard_count * pairwise_heads_sharded * PER_FOCUS_DIM
    )
    attention_result = jnp.concatenate([alignment_flattened, pair_flattened], axis=1)
    alignment_width = sequence_shard_count * alignment_heads_sharded * PER_FOCUS_DIM
    alignment_local = jnp.transpose(
        attention_result[:, :alignment_width].reshape(
            length_value, sequence_shard_count, alignment_heads_sharded * PER_FOCUS_DIM
        ),
        (1, 0, 2),
    )
    pair_local = jnp.transpose(
        attention_result[:, alignment_width:].reshape(
            length_value, residue_shard_count, pairwise_heads_sharded * PER_FOCUS_DIM
        ),
        (1, 0, 2),
    )
    lineup_focus_split, pairwise_heads = (
        lax.all_gather(alignment_local, "head", axis=2, tiled=True),
        lax.all_gather(pair_local, "head", axis=2, tiled=True),
    )
    outer_factors = jnp.einsum(
        "juf,bfn->bjun", alignment_normed, left_right_maps, preferred_element_type=jnp.float32
    )
    outer_factors = (outer_factors * mask_own[None, :, :, None]).astype(jnp.bfloat16)
    factor_rows = lax.all_to_all(
        outer_factors[0], ("rows", "branch"), split_axis=1, concat_axis=0, tiled=True
    )
    col_factors = lax.all_gather(outer_factors[1], ("rows", "branch"), axis=0, tiled=True)
    mask_rows = lax.dynamic_slice_in_dim(mask_full, row_start, residue_shard_count, 1)
    pair_count = jnp.dot(mask_rows.T, mask_full, precision=lax.Precision.HIGHEST)
    col_block = math.gcd(length_value, 128)

    def outer_block(col_start):
        block_cols = lax.dynamic_slice_in_dim(col_factors, col_start, col_block, 1)
        outer_sum = lax.dot_general(
            factor_rows, block_cols, (((0,), (0,)), ((), ())), preferred_element_type=jnp.float32
        )
        counts = lax.dynamic_slice_in_dim(pair_count, col_start, col_block, 1)
        outer_mean = (outer_sum / counts[:, None, :, None]).astype(jnp.bfloat16)
        outer_mean = jnp.transpose(outer_mean, (0, 2, 1, 3)).reshape(
            residue_shard_count * col_block, -1
        )
        return jnp.dot(
            outer_mean, outer_product_output_matrix, preferred_element_type=jnp.float32
        ).reshape(residue_shard_count, col_block, -1)

    starts = jnp.arange(length_value // col_block, dtype=jnp.int32) * col_block
    opm_blocks = lax.map(outer_block, starts)
    opm_update = jnp.transpose(opm_blocks, (1, 0, 2, 3)).reshape(
        residue_shard_count, length_value, -1
    )
    width_z = pair_output_matrix.shape[1]
    tri_update = jnp.dot(
        pairwise_heads.reshape(residue_shard_count * length_value, -1),
        pair_output_matrix,
        preferred_element_type=jnp.float32,
    ).reshape(residue_shard_count, length_value, width_z)
    pair_own = lax.dynamic_slice_in_dim(pairwise, head_location * width_z, width_z, 2).astype(
        jnp.float32
    )
    pairwise_out = (pair_own + tri_update + opm_update).astype(jnp.bfloat16)
    channels = lineup_state.shape[2]
    lineup_blended = lineup_state.astype(jnp.float32) + jnp.dot(
        lineup_focus_split.reshape(sequence_shard_count * length_value, -1),
        lineup_readout_weight,
        preferred_element_type=jnp.float32,
    ).reshape(sequence_shard_count, length_value, channels)
    feedfwd_standardized = layer_normalize(lineup_blended).astype(jnp.bfloat16)
    head_count = lax.axis_size("head")
    hidden = jax.nn.relu(
        jnp.einsum(
            "src,cf->srf",
            feedfwd_standardized,
            feedfwd_entry_weight,
            preferred_element_type=jnp.float32,
        )
    ).astype(jnp.bfloat16)
    partial_value = jnp.einsum(
        "srf,fc->src", hidden, feedfwd_exit_weight, preferred_element_type=jnp.float32
    )
    summed_result = lax.psum_scatter(
        partial_value.astype(jnp.bfloat16), "head", scatter_dimension=2, tiled=True
    ).astype(jnp.float32)
    alignment_channel_width = channels // head_count
    alignment_owned = lax.dynamic_slice_in_dim(
        lineup_blended, head_location * alignment_channel_width, alignment_channel_width, 2
    )
    refreshed_lineup_state = (alignment_owned + summed_result).astype(jnp.bfloat16)
    return (refreshed_lineup_state, pairwise_out)


F32 = jnp.float32
BF16 = jnp.bfloat16
NEG = -1000000000.0
HD = PER_FOCUS_DIM
NI = 14
LOAD_ORDER = (1, 4, 5, 0, 2, 12, 10, 6, 13, 3, 7, 8, 9, 11)


def dot_nt(a, b):
    return lax.dot_general(a, b, (((1,), (1,)), ((), ())), preferred_element_type=F32)


def dot_nn(a, b):
    return jnp.dot(a, b, preferred_element_type=F32)


def head_mask(width, head):
    lanes = lax.broadcasted_iota(jnp.int32, (1, width), 1)
    return jnp.where((lanes >= head * HD) & (lanes < (head + 1) * HD), 1.0, 0.0)


def block_kernel(
    N,
    NB,
    S,
    R,
    L,
    *refs,
):
    hbm = refs[:NI]
    out_m, out_z = refs[NI : NI + 2]
    held = refs[NI + 2 : 2 * NI + 2]
    in_sem = refs[2 * NI + 2]
    loads = [pltpu.make_async_copy(hbm[i], held[i], in_sem.at[i]) for i in range(NI)]
    for i in LOAD_ORDER:
        loads[i].start()
    (
    x_ref,
    z_ref,
    bv_ref,
    val_ref,
    cw_ref,
    tw_ref,
    ap_ref,
    wr_ref,
    we_ref,
    wx_ref,
    pp_ref,
    po_ref,
    lr_ref,
    ow_ref,
    ) = held
    (
    pn,
    xn,
    wscr,
    mscr,
    bscr,
    bias_all,
    b_all,
    a_send,
    a_all,
    bias_f,
    q_s,
    k_s,
    v_s,
    g_s,
    pq_s,
    pk_s,
    pv_s,
    pg_s,
    wf,
    wt,
    bf,
    bmat,
    af,
    at,
    omat,
    mh_own,
    mh_oth,
    ph_own,
    ph_oth,
    mid,
    ps_own,
    ps_send,
    ps_recv,
    bias_ss,
    bias_rs,
    b_ss,
    b_rs,
    a_ss,
    a_rs,
    m_ss,
    m_rs,
    p_ss,
    p_rs,
    f_ss,
    f_rs,
    ) = refs[2 * NI + 3 :]

    def need(*names):
        for name in names:
            loads[name].wait()

    part = lax.axis_index("parts")
    row = lax.axis_index("rows")
    core = lax.axis_index("branch")
    h = lax.axis_index("head")
    me = row * NB + core
    HM = cw_ref.shape[0]
    HZ = tw_ref.shape[0]
    H = HM + HZ
    Q = lr_ref.shape[1]
    C = po_ref.shape[0]
    DM = HM * HD
    DZ = HZ * HD
    inv = 1.0 / math.sqrt(HD)

    def peer(d):
        p = lax.rem(me + d, N)
        return p, (part, p // NB, lax.rem(p, NB), h)

    partner = (part, row, core, 1 - h)

    def remote(src, dst, ss, rs, dev):
        return pltpu.make_async_remote_copy(
            src_ref=src,
            dst_ref=dst,
            send_sem=ss,
            recv_sem=rs,
            device_id=dev,
            device_id_type=pl.DeviceIdType.MESH,
        )

    barrier = pltpu.get_barrier_semaphore()

    def greet(d, c):
        pl.semaphore_signal(
            barrier, inc=1, device_id=peer(d)[1], device_id_type=pl.DeviceIdType.MESH
        )
        return c

    lax.fori_loop(1, N, greet, 0)
    pl.semaphore_signal(barrier, inc=1, device_id=partner, device_id_type=pl.DeviceIdType.MESH)

    need(1, 4, 5)
    pn[...] = layer_normalize(z_ref[...]).astype(BF16)
    wscr[...] = jnp.zeros(wscr.shape, F32)
    wscr[0:HM, :] = cw_ref[...].astype(F32)
    wscr[HM:H, :] = tw_ref[...].astype(F32)
    bt = dot_nt(wscr[...].astype(BF16), pn[...])
    for j in range(R):
        bscr[j * 8 : (j + 1) * 8, :] = bt[:, j * L : (j + 1) * L]
    pieces = [bscr[pl.ds(l, R, stride=8), :] for l in range(H)]
    bias_all[me] = jnp.concatenate(pieces, 0).astype(BF16)

    pl.semaphore_wait(barrier, N)

    def send_bias(d, c):
        p, dev = peer(d)
        remote(bias_all.at[me], bias_all.at[me], bias_ss.at[p], bias_rs.at[me], dev).start()
        return c

    lax.fori_loop(1, N, send_bias, 0)

    need(0, 2, 12)
    xn[...] = layer_normalize(x_ref[...]).astype(BF16)
    wscr[...] = jnp.zeros(wscr.shape, F32)
    wscr[0:2, 0 : N * S] = bv_ref[...].astype(F32)
    bounds = wscr[...].T[0 : N * S]
    lo_v = bounds[:, 0:1]
    hi_v = bounds[:, 1:2]
    lanes = lax.broadcasted_iota(jnp.int32, (N * S, L), 1)
    place = lanes.astype(F32)
    m_all = jnp.where((place >= lo_v) & (place < hi_v), 1.0, 0.0)
    place = (lanes + me * R).astype(F32)
    m_own = jnp.where((place >= lo_v) & (place < hi_v), 1.0, 0.0)
    mscr[0 : N * S, :] = m_all
    mscr[N * S :, :] = jnp.zeros((8, L), F32)
    ft = dot_nt(lr_ref[1], xn[...])
    fa = dot_nt(xn[...], lr_ref[0])
    own_mask = []
    parts_a = []
    for s in range(S):
        inside = mscr[pl.ds(me * S + s, 1), :]
        own_mask.append(inside > 0)
        b_all[me, s * Q : (s + 1) * Q, :] = (ft[:, s * L : (s + 1) * L] * inside).astype(BF16)
        column = jnp.broadcast_to(inside, (8, L)).T[:, 0:1]
        parts_a.append(fa[s * L : (s + 1) * L] * column)
    for p in range(N):
        a_send[p] = jnp.concatenate(
            [parts_a[s][p * R : (p + 1) * R] for s in range(S)], 0
        ).astype(BF16)
    a_all[me] = a_send[me]

    def send_factors(d, c):
        p, dev = peer(d)
        remote(b_all.at[me], b_all.at[me], b_ss.at[p], b_rs.at[me], dev).start()
        remote(a_send.at[p], a_all.at[me], a_ss.at[p], a_rs.at[me], dev).start()
        return c

    lax.fori_loop(1, N, send_factors, 0)

    need(6, 10)
    for g, ref in ((0, q_s), (1, k_s), (2, v_s)):
        ref[...] = dot_nn(xn[...], ap_ref[g]).astype(BF16)
    g_s[...] = jax.nn.sigmoid(dot_nn(xn[...], ap_ref[3]))
    for g, ref in ((0, pq_s), (1, pk_s), (2, pv_s)):
        ref[...] = dot_nt(pn[...], pp_ref[g]).astype(BF16)
    pg_s[...] = jax.nn.sigmoid(dot_nt(pn[...], pp_ref[3]))

    need(13, 3)
    wf[...] = ow_ref[...].astype(F32).T
    for q in range(Q):
        wt[q * Q : (q + 1) * Q, :] = wf[pl.ds(q, Q, stride=Q), :].astype(BF16)

    counts = dot_nn(m_own.T[0:R].astype(BF16), m_all.astype(BF16))
    inv_counts = 1.0 / counts

    def wait_bias(d, c):
        p, dev = peer(d)
        remote(bias_all.at[p], bias_all.at[p], bias_ss.at[p], bias_rs.at[p], dev).wait_recv()
        return c

    lax.fori_loop(1, N, wait_bias, 0)
    valid = val_ref[...] > 0
    for p in range(N):
        piece = bias_all[p].astype(F32)
        for l in range(H):
            sub = piece[l * R : (l + 1) * R]
            if l >= HM:
                sub = jnp.where(valid, sub, NEG)
            bias_f[l * L + p * R : l * L + (p + 1) * R, :] = sub

    mm = [head_mask(DM, i).astype(BF16) for i in range(HM)]
    m_copies = []
    for s in range(S):
        sl = slice(s * L, (s + 1) * L)
        q = q_s[sl]
        v = v_s[sl]
        stack = jnp.concatenate([q * m for m in mm], 0)
        score = dot_nt(stack, k_s[sl]) * inv + bias_f[0 : HM * L, :]
        score = jnp.where(own_mask[s], score, NEG)
        w = jnp.exp(score - jnp.max(score, -1, keepdims=True)).astype(BF16)
        w = jnp.concatenate([w[i * L : (i + 1) * L] for i in range(HM)], 1)
        vv = jnp.concatenate(
            [jnp.concatenate([v * m, jnp.broadcast_to(m, v.shape)], 1) for m in mm], 0
        )
        o = dot_nn(w, vv)
        mh_own[sl] = (o[:, :DM] / o[:, DM:] * g_s[sl]).astype(BF16)
        copy = remote(mh_own.at[sl], mh_oth.at[sl], m_ss.at[s], m_rs.at[s], partner)
        copy.start()
        m_copies.append(copy)

    zm = [head_mask(DZ, i).astype(BF16) for i in range(HZ)]

    def tri(i):
        sl = slice(i * L, (i + 1) * L)
        q = pq_s[sl]
        v = pv_s[sl]
        stack = jnp.concatenate([q * m for m in zm], 0)
        score = dot_nt(stack, pk_s[sl]) * inv + bias_f[HM * L :, :]
        w = jnp.exp(score - jnp.max(score, -1, keepdims=True)).astype(BF16)
        w = jnp.concatenate([w[j * L : (j + 1) * L] for j in range(HZ)], 1)
        vv = jnp.concatenate(
            [jnp.concatenate([v * m, jnp.broadcast_to(m, v.shape)], 1) for m in zm], 0
        )
        o = dot_nn(w, vv)
        return o[:, :DZ] / o[:, DZ:] * pg_s[sl]

    half = R // 2
    p_copies = []
    for i in range(half):
        sl = slice(i * L, (i + 1) * L)
        ph_own[sl] = jnp.concatenate([tri(i), tri(i + half)], 1).astype(BF16)
        copy = remote(ph_own.at[sl], ph_oth.at[sl], p_ss.at[i], p_rs.at[i], partner)
        copy.start()
        p_copies.append(copy)

    need(7, 8, 9, 11)
    for copy in m_copies:
        copy.wait_recv()
    w_own = wr_ref[pl.ds(pl.multiple_of(h * DM, DM), DM), :]
    w_oth = wr_ref[pl.ds(pl.multiple_of((1 - h) * DM, DM), DM), :]
    mid[...] = x_ref[...].astype(F32) + dot_nn(mh_own[...], w_own) + dot_nn(mh_oth[...], w_oth)
    tn = layer_normalize(mid[...]).astype(BF16)
    hidden = jnp.maximum(dot_nn(tn, we_ref[...]), 0.0).astype(BF16)
    W = out_m.shape[1]
    sums = dot_nn(hidden, wx_ref[...])
    first = h == 0
    ps_own[...] = jnp.where(first, sums[:, :W], sums[:, W:])
    ps_send[...] = jnp.where(first, sums[:, W:], sums[:, :W]).astype(BF16)
    f_copy = remote(ps_send, ps_recv, f_ss, f_rs, partner)
    f_copy.start()

    def wait_factors(d, c):
        p, dev = peer(d)
        remote(b_all.at[p], b_all.at[p], b_ss.at[p], b_rs.at[p], dev).wait_recv()
        remote(a_send.at[p], a_all.at[p], a_ss.at[p], a_rs.at[p], dev).wait_recv()
        return c

    lax.fori_loop(1, N, wait_factors, 0)
    SQ = S * Q
    SR = S * R
    for p in range(N):
        bf[p * SQ : (p + 1) * SQ, :] = b_all[p].astype(F32)
        af[p * SR : (p + 1) * SR, :] = a_all[p].astype(F32)
    for q in range(Q):
        bmat[:, q * L : (q + 1) * L] = bf[pl.ds(q, N * S, stride=Q), :].astype(BF16)
    for i in range(R):
        at[i * Q : (i + 1) * Q, :] = af[pl.ds(i, N * S, stride=R), :].T.astype(BF16)
    step = 8
    for q0 in range(0, Q, step):
        o = dot_nn(at[...], bmat[:, q0 * L : (q0 + step) * L]).astype(BF16)
        for q in range(step):
            for i in range(R):
                omat[(q0 + q) * Q : (q0 + q + 1) * Q, i * L : (i + 1) * L] = o[
                    i * Q : (i + 1) * Q, q * L : (q + 1) * L
                ]
    res = dot_nn(wt[...].astype(F32).T.astype(BF16), omat[...])

    po = po_ref[...]
    turned = jnp.concatenate([po[:, DZ:], po[:, :DZ]], 1)
    own_first = jnp.where(first, po, turned)
    oth_first = jnp.where(first, turned, po)
    zl = lax.broadcasted_iota(jnp.int32, (1, 2 * DZ), 1)
    low = jnp.where(zl < DZ, 1.0, 0.0).astype(BF16)
    high = jnp.where(zl >= DZ, 1.0, 0.0).astype(BF16)
    lowers = [own_first * low, oth_first * low]
    uppers = [oth_first * high, own_first * high]
    cc = lax.broadcasted_iota(jnp.int32, (C, 2 * C), 0) + h * C
    pick = jnp.where(cc == lax.broadcasted_iota(jnp.int32, (C, 2 * C), 1), 1.0, 0.0).astype(BF16)
    for copy in p_copies:
        copy.wait_recv()
    for i in range(R):
        k = i % half
        sl = slice(k * L, (k + 1) * L)
        ws = lowers if i < half else uppers
        total = (
            dot_nt(ws[0], ph_own[sl])
            + dot_nt(ws[1], ph_oth[sl])
            + dot_nt(pick, z_ref[i * L : (i + 1) * L, :])
        )
        opm = res[:, i * L : (i + 1) * L] * inv_counts[i : i + 1, :]
        out_z[i] = (total + opm).astype(BF16)

    f_copy.wait_recv()
    out_m[...] = (
        mid[:, pl.ds(pl.multiple_of(h * W, W), W)] + ps_own[...] + ps_recv[...].astype(F32)
    ).astype(BF16)

    def drain(d, c):
        p, dev = peer(d)
        remote(bias_all.at[me], bias_all.at[me], bias_ss.at[p], bias_rs.at[me], dev).wait_send()
        remote(b_all.at[me], b_all.at[me], b_ss.at[p], b_rs.at[me], dev).wait_send()
        remote(a_send.at[p], a_all.at[me], a_ss.at[p], a_rs.at[me], dev).wait_send()
        return c

    lax.fori_loop(1, N, drain, 0)
    for copy in m_copies + p_copies + [f_copy]:
        copy.wait_send()


def fused(N, NB, *args):
    x, z, bounds, valid, cw, tw, ap, wr, we, wx, pp, po, lr, ow = args
    S, L, D = x.shape
    R, _, CZ = z.shape
    HM, HZ = cw.shape[1], tw.shape[1]
    H = HM + HZ
    Q = lr.shape[2]
    C = po.shape[1]
    DM, DZ = HM * HD, HZ * HD
    W = D // 2
    vmem = pl.BlockSpec(memory_space=pltpu.VMEM)
    dma = pltpu.SemaphoreType.DMA
    scratch = [
        pltpu.VMEM((R * L, CZ), BF16),
        pltpu.VMEM((S * L, D), BF16),
        pltpu.VMEM((8, 128), F32),
        pltpu.VMEM((N * S + 8, L), F32),
        pltpu.VMEM((R * 8, L), F32),
        pltpu.VMEM((N, H * R, L), BF16),
        pltpu.VMEM((N, S * Q, L), BF16),
        pltpu.VMEM((N, S * R, Q), BF16),
        pltpu.VMEM((N, S * R, Q), BF16),
        pltpu.VMEM((H * L, L), F32),
        pltpu.VMEM((S * L, DM), BF16),
        pltpu.VMEM((S * L, DM), BF16),
        pltpu.VMEM((S * L, DM), BF16),
        pltpu.VMEM((S * L, DM), F32),
        pltpu.VMEM((R * L, DZ), BF16),
        pltpu.VMEM((R * L, DZ), BF16),
        pltpu.VMEM((R * L, DZ), BF16),
        pltpu.VMEM((R * L, DZ), F32),
        pltpu.VMEM((Q * Q, C), F32),
        pltpu.VMEM((Q * Q, C), BF16),
        pltpu.VMEM((N * S * Q, L), F32),
        pltpu.VMEM((N * S, Q * L), BF16),
        pltpu.VMEM((N * S * R, Q), F32),
        pltpu.VMEM((R * Q, N * S), BF16),
        pltpu.VMEM((Q * Q, R * L), BF16),
        pltpu.VMEM((S * L, DM), BF16),
        pltpu.VMEM((S * L, DM), BF16),
        pltpu.VMEM((R // 2 * L, 2 * DZ), BF16),
        pltpu.VMEM((R // 2 * L, 2 * DZ), BF16),
        pltpu.VMEM((S * L, D), F32),
        pltpu.VMEM((S * L, W), F32),
        pltpu.VMEM((S * L, W), BF16),
        pltpu.VMEM((S * L, W), BF16),
        dma((N,)),
        dma((N,)),
        dma((N,)),
        dma((N,)),
        dma((N,)),
        dma((N,)),
        dma((S,)),
        dma((S,)),
        dma((R // 2,)),
        dma((R // 2,)),
        dma,
        dma,
    ]
    operands = (
        x.reshape(S * L, D),
        z.reshape(R * L, CZ),
        bounds.T,
        valid.reshape(1, L),
        cw.T,
        tw.T,
        ap,
        wr,
        we,
        wx,
        jnp.transpose(pp, (0, 2, 1)),
        po.T,
        jnp.transpose(lr, (0, 2, 1)),
        ow.T,
    )
    held = [pltpu.VMEM(a.shape, a.dtype) for a in operands]
    out_m, out_z = pl.pallas_call(
        functools.partial(block_kernel, N, NB, S, R, L),
        out_shape=(
            jax.ShapeDtypeStruct((S * L, W), BF16),
            jax.ShapeDtypeStruct((R, C, L), BF16),
        ),
        in_specs=[pl.BlockSpec(memory_space=pltpu.HBM)] * NI,
        out_specs=(vmem, vmem),
        scratch_shapes=held + [dma((NI,))] + scratch,
        compiler_params=pltpu.CompilerParams(
            collective_id=0, has_side_effects=True, vmem_limit_bytes=60 * 1024 * 1024
        ),
    )(*operands)
    return out_m.reshape(S, L, W), jnp.transpose(out_z, (0, 2, 1))


def block(N, NB, NH, *args):
    x, z = args[0], args[1]
    S, L, D = x.shape
    if NH == 2 and L == 128 and z.shape[0] == 8 and S == 2 and D == 256:
        return fused(N, NB, *args)
    return local(*args)


def solution(mesh):
    NB = mesh.shape["branch"]
    N = mesh.shape["rows"] * NB
    in_specs = (
        P(("parts", "rows", "branch"), None, None),
        P(("parts", "rows", "branch"), None, None),
        P("parts", None),
        P("parts"),
        P(None, "head"),
        P(None, "head"),
        P(None, None, "head"),
        P(),
        P(None, "head"),
        P("head", None),
        P(None, None, "head"),
        P(None, "head"),
        P(),
        P(None, "head"),
    )
    out_specs = (
        P(("parts", "rows", "branch"), None, "head"),
        P(("parts", "rows", "branch"), None, "head"),
    )
    return jax.shard_map(
        functools.partial(block, N, NB, mesh.shape["head"]), mesh=mesh, in_specs=in_specs, out_specs=out_specs, check_vma=False)
```

```python
import functools
import math

import jax
import jax.numpy as jnp
from jax import lax
from jax.experimental import pallas as pl
from jax.experimental.pallas import tpu as pltpu
from jax.sharding import PartitionSpec as P

PER_FOCUS_DIM = 32


def layer_normalize(values):
    values = values.astype(jnp.float32)
    center = values - jnp.mean(values, -1, keepdims=True)
    spread = jnp.mean(center * center, -1, keepdims=True)
    return center * lax.rsqrt(spread + 1e-05)


def soft_weights(attention_scores):
    row_max = jnp.max(attention_scores, -1, keepdims=True)
    shifted = jnp.exp(attention_scores - row_max)
    return (shifted / jnp.sum(shifted, -1, keepdims=True)).astype(jnp.bfloat16)


def span_mask(aligned_residue_bounds, length_value):
    places = jnp.arange(length_value, dtype=jnp.int32)
    inside = (places[None, :] >= aligned_residue_bounds[:, 0:1]) & (
        places[None, :] < aligned_residue_bounds[:, 1:2]
    )
    return inside.astype(jnp.float32)


def local(
    lineup_state,
    pairwise,
    aligned_residue_bounds,
    residue_valid_mask,
    coupling_offset_weight_map,
    triangle_bias_matrix,
    alignment_projection_matrix,
    lineup_readout_weight,
    feedfwd_entry_weight,
    feedfwd_exit_weight,
    pair_projection_matrix,
    pair_output_matrix,
    left_right_maps,
    outer_product_output_matrix,
):
    sequence_shard_count = lineup_state.shape[0]
    length_value = lineup_state.shape[1]
    residue_shard_count = pairwise.shape[0]
    alignment_heads_sharded = coupling_offset_weight_map.shape[1]
    pairwise_heads_sharded = triangle_bias_matrix.shape[1]
    inv_scale = 1.0 / math.sqrt(PER_FOCUS_DIM)
    row_place = lax.axis_index(("rows", "branch"))
    head_location = lax.axis_index("head")
    seq_start = row_place * sequence_shard_count
    row_start = row_place * residue_shard_count
    mask_full = span_mask(aligned_residue_bounds, length_value)
    mask_own = lax.dynamic_slice_in_dim(mask_full, seq_start, sequence_shard_count, 0)
    key_valid = residue_valid_mask > 0
    alignment_normed = layer_normalize(lineup_state).astype(jnp.bfloat16)
    pair_normed = layer_normalize(pairwise).astype(jnp.bfloat16)
    bias_matrix = jnp.concatenate([coupling_offset_weight_map, triangle_bias_matrix], axis=1)
    bias_local = jnp.einsum(
        "tue,el->ltu", pair_normed, bias_matrix, preferred_element_type=jnp.float32
    ).astype(jnp.bfloat16)
    lineup_mapped = jnp.einsum(
        "tvf,xfp->xtvp",
        alignment_normed,
        alignment_projection_matrix,
        preferred_element_type=jnp.float32,
    )
    lineup_probe_lookup_content = (
        lineup_mapped[:3]
        .astype(jnp.bfloat16)
        .reshape(3, sequence_shard_count, length_value, alignment_heads_sharded, PER_FOCUS_DIM)
    )
    alignment_gate = jax.nn.sigmoid(lineup_mapped[3])
    pair_proj = jnp.einsum(
        "ijc,gcd->gijd", pair_normed, pair_projection_matrix, preferred_element_type=jnp.float32
    )
    pair_qkv = (
        pair_proj[:3]
        .astype(jnp.bfloat16)
        .reshape(3, residue_shard_count, length_value, pairwise_heads_sharded, PER_FOCUS_DIM)
    )
    pair_gate = jax.nn.sigmoid(pair_proj[3])
    bias_portion = lax.all_gather(bias_local, ("rows", "branch"), axis=1, tiled=True)
    row_total_count = bias_portion.shape[1]
    alignment_query = lineup_probe_lookup_content[0]
    attention_scores = (
        jnp.einsum(
            "xtza,xfza->xztf",
            alignment_query,
            lineup_probe_lookup_content[1],
            preferred_element_type=jnp.float32,
        )
        * inv_scale
    )
    attention_scores = (
        attention_scores + bias_portion[:alignment_heads_sharded].astype(jnp.float32)[None]
    )
    attention_scores = jnp.where(mask_own[:, None, None, :] > 0, attention_scores, -1000000000.0)
    softmax_shares = soft_weights(attention_scores)
    alignment_portion = jnp.einsum(
        "fxkc,fcxz->fkxz",
        softmax_shares,
        lineup_probe_lookup_content[2],
        preferred_element_type=jnp.float32,
    )
    alignment_portion = alignment_portion.reshape(
        sequence_shard_count, row_total_count, alignment_heads_sharded * PER_FOCUS_DIM
    )
    alignment_portion = (alignment_portion * alignment_gate).astype(jnp.bfloat16)
    pair_query = pair_qkv[0]
    triangle_scores = (
        jnp.einsum("ijhd,ikhd->ihjk", pair_query, pair_qkv[1], preferred_element_type=jnp.float32)
        * inv_scale
    )
    triangle_scores = (
        triangle_scores + bias_portion[alignment_heads_sharded:].astype(jnp.float32)[None]
    )
    triangle_scores = jnp.where(key_valid[None, None, None, :], triangle_scores, -1000000000.0)
    tri_weights = soft_weights(triangle_scores)
    pair_part = jnp.einsum(
        "ihjk,ikhd->ijhd", tri_weights, pair_qkv[2], preferred_element_type=jnp.float32
    )
    pair_part = pair_part.reshape(
        residue_shard_count, row_total_count, pairwise_heads_sharded * PER_FOCUS_DIM
    )
    pair_part = (pair_part * pair_gate).astype(jnp.bfloat16)
    alignment_flattened = jnp.transpose(alignment_portion, (1, 0, 2)).reshape(
        row_total_count, sequence_shard_count * alignment_heads_sharded * PER_FOCUS_DIM
    )
    pair_flattened = jnp.transpose(pair_part, (1, 0, 2)).reshape(
        row_total_count, residue_shard_count * pairwise_heads_sharded * PER_FOCUS_DIM
    )
    attention_result = jnp.concatenate([alignment_flattened, pair_flattened], axis=1)
    alignment_width = sequence_shard_count * alignment_heads_sharded * PER_FOCUS_DIM
    alignment_local = jnp.transpose(
        attention_result[:, :alignment_width].reshape(
            length_value, sequence_shard_count, alignment_heads_sharded * PER_FOCUS_DIM
        ),
        (1, 0, 2),
    )
    pair_local = jnp.transpose(
        attention_result[:, alignment_width:].reshape(
            length_value, residue_shard_count, pairwise_heads_sharded * PER_FOCUS_DIM
        ),
        (1, 0, 2),
    )
    lineup_focus_split, pairwise_heads = (
        lax.all_gather(alignment_local, "head", axis=2, tiled=True),
        lax.all_gather(pair_local, "head", axis=2, tiled=True),
    )
    outer_factors = jnp.einsum(
        "juf,bfn->bjun", alignment_normed, left_right_maps, preferred_element_type=jnp.float32
    )
    outer_factors = (outer_factors * mask_own[None, :, :, None]).astype(jnp.bfloat16)
    factor_rows = lax.all_to_all(
        outer_factors[0], ("rows", "branch"), split_axis=1, concat_axis=0, tiled=True
    )
    col_factors = lax.all_gather(outer_factors[1], ("rows", "branch"), axis=0, tiled=True)
    mask_rows = lax.dynamic_slice_in_dim(mask_full, row_start, residue_shard_count, 1)
    pair_count = jnp.dot(mask_rows.T, mask_full, precision=lax.Precision.HIGHEST)
    col_block = math.gcd(length_value, 128)

    def outer_block(col_start):
        block_cols = lax.dynamic_slice_in_dim(col_factors, col_start, col_block, 1)
        outer_sum = lax.dot_general(
            factor_rows, block_cols, (((0,), (0,)), ((), ())), preferred_element_type=jnp.float32
        )
        counts = lax.dynamic_slice_in_dim(pair_count, col_start, col_block, 1)
        outer_mean = (outer_sum / counts[:, None, :, None]).astype(jnp.bfloat16)
        outer_mean = jnp.transpose(outer_mean, (0, 2, 1, 3)).reshape(
            residue_shard_count * col_block, -1
        )
        return jnp.dot(
            outer_mean, outer_product_output_matrix, preferred_element_type=jnp.float32
        ).reshape(residue_shard_count, col_block, -1)

    starts = jnp.arange(length_value // col_block, dtype=jnp.int32) * col_block
    opm_blocks = lax.map(outer_block, starts)
    opm_update = jnp.transpose(opm_blocks, (1, 0, 2, 3)).reshape(
        residue_shard_count, length_value, -1
    )
    width_z = pair_output_matrix.shape[1]
    tri_update = jnp.dot(
        pairwise_heads.reshape(residue_shard_count * length_value, -1),
        pair_output_matrix,
        preferred_element_type=jnp.float32,
    ).reshape(residue_shard_count, length_value, width_z)
    pair_own = lax.dynamic_slice_in_dim(pairwise, head_location * width_z, width_z, 2).astype(
        jnp.float32
    )
    pairwise_out = (pair_own + tri_update + opm_update).astype(jnp.bfloat16)
    channels = lineup_state.shape[2]
    lineup_blended = lineup_state.astype(jnp.float32) + jnp.dot(
        lineup_focus_split.reshape(sequence_shard_count * length_value, -1),
        lineup_readout_weight,
        preferred_element_type=jnp.float32,
    ).reshape(sequence_shard_count, length_value, channels)
    feedfwd_standardized = layer_normalize(lineup_blended).astype(jnp.bfloat16)
    head_count = lax.axis_size("head")
    hidden = jax.nn.relu(
        jnp.einsum(
            "src,cf->srf",
            feedfwd_standardized,
            feedfwd_entry_weight,
            preferred_element_type=jnp.float32,
        )
    ).astype(jnp.bfloat16)
    partial_value = jnp.einsum(
        "srf,fc->src", hidden, feedfwd_exit_weight, preferred_element_type=jnp.float32
    )
    summed_result = lax.psum_scatter(
        partial_value.astype(jnp.bfloat16), "head", scatter_dimension=2, tiled=True
    ).astype(jnp.float32)
    alignment_channel_width = channels // head_count
    alignment_owned = lax.dynamic_slice_in_dim(
        lineup_blended, head_location * alignment_channel_width, alignment_channel_width, 2
    )
    refreshed_lineup_state = (alignment_owned + summed_result).astype(jnp.bfloat16)
    return (refreshed_lineup_state, pairwise_out)


F32 = jnp.float32
BF16 = jnp.bfloat16
NEG = -1000000000.0
HD = PER_FOCUS_DIM
NI = 14
LOAD_ORDER = (1, 4, 5, 0, 2, 12, 10, 6, 13, 3, 7, 8, 9, 11)


def dot_nt(a, b):
    return lax.dot_general(a, b, (((1,), (1,)), ((), ())), preferred_element_type=F32)


def dot_nn(a, b):
    return jnp.dot(a, b, preferred_element_type=F32)


def head_mask(width, head):
    lanes = lax.broadcasted_iota(jnp.int32, (1, width), 1)
    return jnp.where((lanes >= head * HD) & (lanes < (head + 1) * HD), 1.0, 0.0)


def block_kernel(
    N,
    NB,
    S,
    R,
    L,
    *refs,
):
    hbm = refs[:NI]
    out_m, out_z = refs[NI : NI + 2]
    held = refs[NI + 2 : 2 * NI + 2]
    in_sem = refs[2 * NI + 2]
    loads = [pltpu.make_async_copy(hbm[i], held[i], in_sem.at[i]) for i in range(NI)]
    for i in LOAD_ORDER:
        loads[i].start()
    (
    x_ref,
    z_ref,
    bv_ref,
    val_ref,
    cw_ref,
    tw_ref,
    ap_ref,
    wr_ref,
    we_ref,
    wx_ref,
    pp_ref,
    po_ref,
    lr_ref,
    ow_ref,
    ) = held
    (
    pn,
    xn,
    wscr,
    mscr,
    bscr,
    bias_all,
    b_all,
    a_send,
    a_all,
    bias_f,
    q_s,
    k_s,
    v_s,
    g_s,
    pq_s,
    pk_s,
    pv_s,
    pg_s,
    wf,
    wt,
    bf,
    bmat,
    af,
    at,
    omat,
    mh_own,
    mh_oth,
    ph_own,
    ph_oth,
    mid,
    ps_own,
    ps_send,
    ps_recv,
    bias_ss,
    bias_rs,
    b_ss,
    b_rs,
    a_ss,
    a_rs,
    m_ss,
    m_rs,
    p_ss,
    p_rs,
    f_ss,
    f_rs,
    ) = refs[2 * NI + 3 :]

    def need(*names):
        for name in names:
            loads[name].wait()

    part = lax.axis_index("parts")
    row = lax.axis_index("rows")
    core = lax.axis_index("branch")
    h = lax.axis_index("head")
    me = row * NB + core
    HM = cw_ref.shape[0]
    HZ = tw_ref.shape[0]
    H = HM + HZ
    Q = lr_ref.shape[1]
    C = po_ref.shape[0]
    DM = HM * HD
    DZ = HZ * HD
    inv = 1.0 / math.sqrt(HD)

    def peer(d):
        p = lax.rem(me + d, N)
        return p, (part, p // NB, lax.rem(p, NB), h)

    partner = (part, row, core, 1 - h)
    NR = N // NB
    sibling = (part, row, 1 - core, h)
    twin = row * NB + 1 - core

    def same_core(d):
        r = lax.rem(row + d, NR)
        return r * NB + core, r * NB + 1 - core, (part, r, core, h)

    def spread(buf, ss, rs):
        def one(d, c):
            p, _, dev = same_core(d)
            remote(buf.at[me], buf.at[me], ss.at[p], rs.at[me], dev).start()
            return c

        lax.fori_loop(1, NR, one, 0)
        remote(buf.at[me], buf.at[me], ss.at[twin], rs.at[me], sibling).start()

    def forward(buf, ss, rs):
        def one(d, c):
            p, t, dev = same_core(d)
            remote(buf.at[p], buf.at[p], ss.at[p], rs.at[p], dev).wait_recv()
            remote(buf.at[p], buf.at[p], ss.at[t], rs.at[p], sibling).start()
            return c

        lax.fori_loop(1, NR, one, 0)

    def collect(buf, ss, rs):
        def one(d, c):
            _, t, _ = same_core(d)
            remote(buf.at[t], buf.at[t], ss.at[t], rs.at[t], sibling).wait_recv()
            return c

        lax.fori_loop(0, NR, one, 0)

    def finish(buf, ss, rs):
        def one(d, c):
            p, t, dev = same_core(d)
            remote(buf.at[me], buf.at[me], ss.at[p], rs.at[me], dev).wait_send()
            remote(buf.at[p], buf.at[p], ss.at[t], rs.at[p], sibling).wait_send()
            return c

        lax.fori_loop(1, NR, one, 0)
        remote(buf.at[me], buf.at[me], ss.at[twin], rs.at[me], sibling).wait_send()

    def remote(src, dst, ss, rs, dev):
        return pltpu.make_async_remote_copy(
            src_ref=src,
            dst_ref=dst,
            send_sem=ss,
            recv_sem=rs,
            device_id=dev,
            device_id_type=pl.DeviceIdType.MESH,
        )

    barrier = pltpu.get_barrier_semaphore()

    def greet(d, c):
        pl.semaphore_signal(
            barrier, inc=1, device_id=peer(d)[1], device_id_type=pl.DeviceIdType.MESH
        )
        return c

    lax.fori_loop(1, N, greet, 0)
    pl.semaphore_signal(barrier, inc=1, device_id=partner, device_id_type=pl.DeviceIdType.MESH)

    need(1, 4, 5)
    pn[...] = layer_normalize(z_ref[...]).astype(BF16)
    wscr[...] = jnp.zeros(wscr.shape, F32)
    wscr[0:HM, :] = cw_ref[...].astype(F32)
    wscr[HM:H, :] = tw_ref[...].astype(F32)
    bt = dot_nt(wscr[...].astype(BF16), pn[...])
    for j in range(R):
        bscr[j * 8 : (j + 1) * 8, :] = bt[:, j * L : (j + 1) * L]
    pieces = [bscr[pl.ds(l, R, stride=8), :] for l in range(H)]
    bias_all[me] = jnp.concatenate(pieces, 0).astype(BF16)

    pl.semaphore_wait(barrier, N)

    spread(bias_all, bias_ss, bias_rs)

    need(0, 2, 12)
    xn[...] = layer_normalize(x_ref[...]).astype(BF16)
    wscr[...] = jnp.zeros(wscr.shape, F32)
    wscr[0:2, 0 : N * S] = bv_ref[...].astype(F32)
    bounds = wscr[...].T[0 : N * S]
    lo_v = bounds[:, 0:1]
    hi_v = bounds[:, 1:2]
    lanes = lax.broadcasted_iota(jnp.int32, (N * S, L), 1)
    place = lanes.astype(F32)
    m_all = jnp.where((place >= lo_v) & (place < hi_v), 1.0, 0.0)
    place = (lanes + me * R).astype(F32)
    m_own = jnp.where((place >= lo_v) & (place < hi_v), 1.0, 0.0)
    mscr[0 : N * S, :] = m_all
    mscr[N * S :, :] = jnp.zeros((8, L), F32)
    ft = dot_nt(lr_ref[1], xn[...])
    fa = dot_nt(xn[...], lr_ref[0])
    own_mask = []
    parts_a = []
    for s in range(S):
        inside = mscr[pl.ds(me * S + s, 1), :]
        own_mask.append(inside > 0)
        b_all[me, s * Q : (s + 1) * Q, :] = (ft[:, s * L : (s + 1) * L] * inside).astype(BF16)
        column = jnp.broadcast_to(inside, (8, L)).T[:, 0:1]
        parts_a.append(fa[s * L : (s + 1) * L] * column)
    for p in range(N):
        a_send[p] = jnp.concatenate(
            [parts_a[s][p * R : (p + 1) * R] for s in range(S)], 0
        ).astype(BF16)
    a_all[me] = a_send[me]

    spread(b_all, b_ss, b_rs)

    def send_left(d, c):
        p, dev = peer(d)
        remote(a_send.at[p], a_all.at[me], a_ss.at[p], a_rs.at[me], dev).start()
        return c

    lax.fori_loop(1, N, send_left, 0)

    need(6, 10)
    for g, ref in ((0, q_s), (1, k_s), (2, v_s)):
        ref[...] = dot_nn(xn[...], ap_ref[g]).astype(BF16)
    g_s[...] = jax.nn.sigmoid(dot_nn(xn[...], ap_ref[3]))
    for g, ref in ((0, pq_s), (1, pk_s), (2, pv_s)):
        ref[...] = dot_nt(pn[...], pp_ref[g]).astype(BF16)
    pg_s[...] = jax.nn.sigmoid(dot_nt(pn[...], pp_ref[3]))

    need(13, 3)
    wf[...] = ow_ref[...].astype(F32).T
    for q in range(Q):
        wt[q * Q : (q + 1) * Q, :] = wf[pl.ds(q, Q, stride=Q), :].astype(BF16)

    counts = dot_nn(m_own.T[0:R].astype(BF16), m_all.astype(BF16))
    inv_counts = 1.0 / counts

    forward(bias_all, bias_ss, bias_rs)
    collect(bias_all, bias_ss, bias_rs)
    valid = val_ref[...] > 0
    for p in range(N):
        piece = bias_all[p].astype(F32)
        for l in range(H):
            sub = piece[l * R : (l + 1) * R]
            if l >= HM:
                sub = jnp.where(valid, sub, NEG)
            bias_f[l * L + p * R : l * L + (p + 1) * R, :] = sub

    mm = [head_mask(DM, i).astype(BF16) for i in range(HM)]
    m_copies = []
    for s in range(S):
        sl = slice(s * L, (s + 1) * L)
        q = q_s[sl]
        v = v_s[sl]
        stack = jnp.concatenate([q * m for m in mm], 0)
        score = dot_nt(stack, k_s[sl]) * inv + bias_f[0 : HM * L, :]
        score = jnp.where(own_mask[s], score, NEG)
        w = jnp.exp(score - jnp.max(score, -1, keepdims=True)).astype(BF16)
        w = jnp.concatenate([w[i * L : (i + 1) * L] for i in range(HM)], 1)
        vv = jnp.concatenate(
            [jnp.concatenate([v * m, jnp.broadcast_to(m, v.shape)], 1) for m in mm], 0
        )
        o = dot_nn(w, vv)
        mh_own[sl] = (o[:, :DM] / o[:, DM:] * g_s[sl]).astype(BF16)
        copy = remote(mh_own.at[sl], mh_oth.at[sl], m_ss.at[s], m_rs.at[s], partner)
        copy.start()
        m_copies.append(copy)

    zm = [head_mask(DZ, i).astype(BF16) for i in range(HZ)]

    def tri(i):
        sl = slice(i * L, (i + 1) * L)
        q = pq_s[sl]
        v = pv_s[sl]
        stack = jnp.concatenate([q * m for m in zm], 0)
        score = dot_nt(stack, pk_s[sl]) * inv + bias_f[HM * L :, :]
        w = jnp.exp(score - jnp.max(score, -1, keepdims=True)).astype(BF16)
        w = jnp.concatenate([w[j * L : (j + 1) * L] for j in range(HZ)], 1)
        vv = jnp.concatenate(
            [jnp.concatenate([v * m, jnp.broadcast_to(m, v.shape)], 1) for m in zm], 0
        )
        o = dot_nn(w, vv)
        return o[:, :DZ] / o[:, DZ:] * pg_s[sl]

    half = R // 2
    p_copies = []
    for i in range(half):
        sl = slice(i * L, (i + 1) * L)
        ph_own[sl] = jnp.concatenate([tri(i), tri(i + half)], 1).astype(BF16)
        copy = remote(ph_own.at[sl], ph_oth.at[sl], p_ss.at[i], p_rs.at[i], partner)
        copy.start()
        p_copies.append(copy)

    forward(b_all, b_ss, b_rs)

    need(7, 8, 9, 11)
    for copy in m_copies:
        copy.wait_recv()
    w_own = wr_ref[pl.ds(pl.multiple_of(h * DM, DM), DM), :]
    w_oth = wr_ref[pl.ds(pl.multiple_of((1 - h) * DM, DM), DM), :]
    mid[...] = x_ref[...].astype(F32) + dot_nn(mh_own[...], w_own) + dot_nn(mh_oth[...], w_oth)
    tn = layer_normalize(mid[...]).astype(BF16)
    hidden = jnp.maximum(dot_nn(tn, we_ref[...]), 0.0).astype(BF16)
    W = out_m.shape[1]
    sums = dot_nn(hidden, wx_ref[...])
    first = h == 0
    ps_own[...] = jnp.where(first, sums[:, :W], sums[:, W:])
    ps_send[...] = jnp.where(first, sums[:, W:], sums[:, :W]).astype(BF16)
    f_copy = remote(ps_send, ps_recv, f_ss, f_rs, partner)
    f_copy.start()

    collect(b_all, b_ss, b_rs)

    def wait_left(d, c):
        p, dev = peer(d)
        remote(a_send.at[p], a_all.at[p], a_ss.at[p], a_rs.at[p], dev).wait_recv()
        return c

    lax.fori_loop(1, N, wait_left, 0)
    SQ = S * Q
    SR = S * R
    for p in range(N):
        bf[p * SQ : (p + 1) * SQ, :] = b_all[p].astype(F32)
        af[p * SR : (p + 1) * SR, :] = a_all[p].astype(F32)
    for q in range(Q):
        bmat[:, q * L : (q + 1) * L] = bf[pl.ds(q, N * S, stride=Q), :].astype(BF16)
    for i in range(R):
        at[i * Q : (i + 1) * Q, :] = af[pl.ds(i, N * S, stride=R), :].T.astype(BF16)
    step = 8
    for q0 in range(0, Q, step):
        o = dot_nn(at[...], bmat[:, q0 * L : (q0 + step) * L]).astype(BF16)
        for q in range(step):
            for i in range(R):
                omat[(q0 + q) * Q : (q0 + q + 1) * Q, i * L : (i + 1) * L] = o[
                    i * Q : (i + 1) * Q, q * L : (q + 1) * L
                ]
    res = dot_nn(wt[...].astype(F32).T.astype(BF16), omat[...])

    po = po_ref[...]
    turned = jnp.concatenate([po[:, DZ:], po[:, :DZ]], 1)
    own_first = jnp.where(first, po, turned)
    oth_first = jnp.where(first, turned, po)
    zl = lax.broadcasted_iota(jnp.int32, (1, 2 * DZ), 1)
    low = jnp.where(zl < DZ, 1.0, 0.0).astype(BF16)
    high = jnp.where(zl >= DZ, 1.0, 0.0).astype(BF16)
    lowers = [own_first * low, oth_first * low]
    uppers = [oth_first * high, own_first * high]
    cc = lax.broadcasted_iota(jnp.int32, (C, 2 * C), 0) + h * C
    pick = jnp.where(cc == lax.broadcasted_iota(jnp.int32, (C, 2 * C), 1), 1.0, 0.0).astype(BF16)
    for copy in p_copies:
        copy.wait_recv()
    for i in range(R):
        k = i % half
        sl = slice(k * L, (k + 1) * L)
        ws = lowers if i < half else uppers
        total = (
            dot_nt(ws[0], ph_own[sl])
            + dot_nt(ws[1], ph_oth[sl])
            + dot_nt(pick, z_ref[i * L : (i + 1) * L, :])
        )
        opm = res[:, i * L : (i + 1) * L] * inv_counts[i : i + 1, :]
        out_z[i] = (total + opm).astype(BF16)

    f_copy.wait_recv()
    out_m[...] = (
        mid[:, pl.ds(pl.multiple_of(h * W, W), W)] + ps_own[...] + ps_recv[...].astype(F32)
    ).astype(BF16)

    finish(bias_all, bias_ss, bias_rs)
    finish(b_all, b_ss, b_rs)

    def drain(d, c):
        p, dev = peer(d)
        remote(a_send.at[p], a_all.at[me], a_ss.at[p], a_rs.at[me], dev).wait_send()
        return c

    lax.fori_loop(1, N, drain, 0)
    for copy in m_copies + p_copies + [f_copy]:
        copy.wait_send()


def fused(N, NB, *args):
    x, z, bounds, valid, cw, tw, ap, wr, we, wx, pp, po, lr, ow = args
    S, L, D = x.shape
    R, _, CZ = z.shape
    HM, HZ = cw.shape[1], tw.shape[1]
    H = HM + HZ
    Q = lr.shape[2]
    C = po.shape[1]
    DM, DZ = HM * HD, HZ * HD
    W = D // 2
    vmem = pl.BlockSpec(memory_space=pltpu.VMEM)
    dma = pltpu.SemaphoreType.DMA
    scratch = [
        pltpu.VMEM((R * L, CZ), BF16),
        pltpu.VMEM((S * L, D), BF16),
        pltpu.VMEM((8, 128), F32),
        pltpu.VMEM((N * S + 8, L), F32),
        pltpu.VMEM((R * 8, L), F32),
        pltpu.VMEM((N, H * R, L), BF16),
        pltpu.VMEM((N, S * Q, L), BF16),
        pltpu.VMEM((N, S * R, Q), BF16),
        pltpu.VMEM((N, S * R, Q), BF16),
        pltpu.VMEM((H * L, L), F32),
        pltpu.VMEM((S * L, DM), BF16),
        pltpu.VMEM((S * L, DM), BF16),
        pltpu.VMEM((S * L, DM), BF16),
        pltpu.VMEM((S * L, DM), F32),
        pltpu.VMEM((R * L, DZ), BF16),
        pltpu.VMEM((R * L, DZ), BF16),
        pltpu.VMEM((R * L, DZ), BF16),
        pltpu.VMEM((R * L, DZ), F32),
        pltpu.VMEM((Q * Q, C), F32),
        pltpu.VMEM((Q * Q, C), BF16),
        pltpu.VMEM((N * S * Q, L), F32),
        pltpu.VMEM((N * S, Q * L), BF16),
        pltpu.VMEM((N * S * R, Q), F32),
        pltpu.VMEM((R * Q, N * S), BF16),
        pltpu.VMEM((Q * Q, R * L), BF16),
        pltpu.VMEM((S * L, DM), BF16),
        pltpu.VMEM((S * L, DM), BF16),
        pltpu.VMEM((R // 2 * L, 2 * DZ), BF16),
        pltpu.VMEM((R // 2 * L, 2 * DZ), BF16),
        pltpu.VMEM((S * L, D), F32),
        pltpu.VMEM((S * L, W), F32),
        pltpu.VMEM((S * L, W), BF16),
        pltpu.VMEM((S * L, W), BF16),
        dma((N,)),
        dma((N,)),
        dma((N,)),
        dma((N,)),
        dma((N,)),
        dma((N,)),
        dma((S,)),
        dma((S,)),
        dma((R // 2,)),
        dma((R // 2,)),
        dma,
        dma,
    ]
    operands = (
        x.reshape(S * L, D),
        z.reshape(R * L, CZ),
        bounds.T,
        valid.reshape(1, L),
        cw.T,
        tw.T,
        ap,
        wr,
        we,
        wx,
        jnp.transpose(pp, (0, 2, 1)),
        po.T,
        jnp.transpose(lr, (0, 2, 1)),
        ow.T,
    )
    held = [pltpu.VMEM(a.shape, a.dtype) for a in operands]
    out_m, out_z = pl.pallas_call(
        functools.partial(block_kernel, N, NB, S, R, L),
        out_shape=(
            jax.ShapeDtypeStruct((S * L, W), BF16),
            jax.ShapeDtypeStruct((R, C, L), BF16),
        ),
        in_specs=[pl.BlockSpec(memory_space=pltpu.HBM)] * NI,
        out_specs=(vmem, vmem),
        scratch_shapes=held + [dma((NI,))] + scratch,
        compiler_params=pltpu.CompilerParams(
            collective_id=0, has_side_effects=True, vmem_limit_bytes=60 * 1024 * 1024
        ),
    )(*operands)
    return out_m.reshape(S, L, W), jnp.transpose(out_z, (0, 2, 1))


def block(N, NB, NH, *args):
    x, z = args[0], args[1]
    S, L, D = x.shape
    if NH == 2 and NB == 2 and L == 128 and z.shape[0] == 8 and S == 2 and D == 256:
        return fused(N, NB, *args)
    return local(*args)


def solution(mesh):
    NB = mesh.shape["branch"]
    N = mesh.shape["rows"] * NB
    in_specs = (
        P(("parts", "rows", "branch"), None, None),
        P(("parts", "rows", "branch"), None, None),
        P("parts", None),
        P("parts"),
        P(None, "head"),
        P(None, "head"),
        P(None, None, "head"),
        P(),
        P(None, "head"),
        P("head", None),
        P(None, None, "head"),
        P(None, "head"),
        P(),
        P(None, "head"),
    )
    out_specs = (
        P(("parts", "rows", "branch"), None, "head"),
        P(("parts", "rows", "branch"), None, "head"),
    )
    return jax.shard_map(
        functools.partial(block, N, NB, mesh.shape["head"]), mesh=mesh, in_specs=in_specs, out_specs=out_specs, check_vma=False)
```
